1024 devices in a mesh: mp: 32 (over x, z_hi, core), replica: 32 (over y, z_lo).
Axes of the slice: x: 8, y: 8, z: 8 (z_hi: 2, z_lo: 4; z = z_hi * 4 + z_lo), core: 2. Of those that a mesh axis runs over, the one named last changes fastest.
Arguments:
- tables: bfloat16 [256, 512, 128], P('mp'), may hold values from -6 to 6
- feature_ids: int32 [24576, 256, 4], P('replica', 'mp'), may hold values from 0 to 511
- bag_lengths: int32 [24576, 256], P('replica', 'mp'), may hold values from 1 to 4
- reduce_weight: bfloat16 [32768, 256], P('mp'), may hold values from -0.03125 to 0.03125
- expand_weight: bfloat16 [32768, 256], P('mp'), may hold values from -0.375 to 0.375
- cross_bias: float32 [32768], P('mp'), may hold values from -3 to 3
- cotangent: bfloat16 [24576, 32768], P('replica', 'mp'), may hold values from -6 to 6
Outputs:
- crossed: bfloat16 [24576, 32768], P('replica', 'mp')
- grad_reduce: float32 [32768, 256], P(('mp', 'replica'))
- grad_expand: float32 [32768, 256], P(('mp', 'replica'))
- grad_bias: float32 [32768], P(('mp', 'replica'))
- grad_tables: float32 [256, 512, 128], P('mp', 'replica')
The draws below stay inside these ranges and needn't reach their ends.
All inputs are finite; a program needn't handle non-finite values.
Results may differ from the reference program's by a relative error of at most 0.0058.
Values may be sent and summed in bfloat16 or wider, within the bound.
A program may use at most 32 MiB of HBM per device.

```python
import math
import jax
import jax.numpy as jnp
import numpy as np
from jax import lax

EMB = 128
RANK = 256
ROWS = 512
HOT = 4
TABLES = 256
FEATURES = 32768
GROUP = 768
SAMPLES = 24576


def place_ends(entries, stream_key, smallest, top_value):
    dims = entries.shape
    spot = [jax.random.randint(jax.random.fold_in(stream_key, axis), (), 0, dims[axis]) for axis in range(len(dims))]
    entries = entries.at[tuple(spot)].set(smallest)
    longest = dims.index(max(dims))
    spot[longest] = (spot[longest] + 1) % dims[longest]
    return entries.at[tuple(spot)].set(top_value)


def levels(rng, extent, split, least, largest):
    def one(position, parts):
        steps = jax.random.uniform(jax.random.fold_in(jax.random.fold_in(rng, 6), position), (parts,), jnp.float32, least / len(split), largest / len(split))
        return jnp.repeat(jnp.exp(steps), extent[position] // parts).reshape((-1,) + (1,) * (len(extent) - position - 1))

    gain = one(*split[0])
    for cut in split[1:]:
        gain = gain * one(*cut)
    return gain


def cumulative_ranks(number_of, skew):
    weights = [(1 << 20) // math.isqrt(standing ** skew) + 1 for standing in range(1, number_of + 1)]
    width = 1 + sum(weights) // (1 << 30)
    return np.cumsum(np.array([max(1, weight // width) for weight in weights]))


def ranked_ids(key, extent, count, lean):
    listing = cumulative_ranks(count, lean)
    ticket = jax.random.randint(jax.random.fold_in(key, 1), extent, 0, int(listing[count - 1]))
    standing = jnp.searchsorted(jnp.asarray(listing, jnp.int32), ticket, side="right")
    return jax.random.permutation(jax.random.fold_in(key, 2), count)[standing].astype(jnp.int32)


def normal_values(rng, dims, spread, limit, cuts=(), kind=jnp.bfloat16):
    result = jax.random.normal(rng, dims, jnp.float32) * spread
    if len(cuts) > 0:
        result = levels(rng, dims, cuts, -0.22, 0.18) * result
    return jnp.clip(result, min=-limit, max=limit).astype(kind)


def setup_inputs(seed: int = 0) -> dict:
    arg_keys = jax.random.split(jax.random.key(seed), 8)
    tables = normal_values(arg_keys[0], (TABLES, ROWS, EMB), 1.0, 6.0, ((0, 32),))
    feature_ids = place_ends(ranked_ids(arg_keys[1], (SAMPLES, TABLES, HOT), ROWS, 2), jax.random.fold_in(arg_keys[1], 3), 0, ROWS - 1).astype(jnp.int32)
    bag_lengths = place_ends(jax.random.randint(arg_keys[2], (SAMPLES, TABLES), 1, HOT + 1), jax.random.fold_in(arg_keys[2], 1), 1, HOT).astype(jnp.int32)
    reduce_weight = normal_values(arg_keys[3], (FEATURES, RANK), FEATURES ** -0.5, 0.03125, ((0, 32),))
    expand_weight = normal_values(arg_keys[4], (FEATURES, RANK), RANK ** -0.5, 0.375, ((0, 32),))
    cross_bias = normal_values(arg_keys[5], (FEATURES,), 0.5, 3.0, ((0, 32),), jnp.float32)
    cotangent = normal_values(arg_keys[6], (SAMPLES, FEATURES), 1.0, 6.0, ((0, 32), (1, 32)))
    return {"tables": tables, "feature_ids": feature_ids, "bag_lengths": bag_lengths, "reduce_weight": reduce_weight, "expand_weight": expand_weight, "cross_bias": cross_bias, "cotangent": cotangent}


def pool_table(table, id_cols, len_col):
    rows = jnp.take(table, id_cols, axis=0).astype(jnp.float32)
    live = jnp.arange(id_cols.shape[1], dtype=jnp.int32)[None, :] < len_col[:, None]
    total = jnp.sum(jnp.where(live[:, :, None], rows, jnp.float32(0.0)), axis=1)
    return total / len_col[:, None].astype(jnp.float32)


def spread_table(grad_cols, id_cols, len_col, row_count):
    live = jnp.arange(id_cols.shape[1], dtype=jnp.int32)[None, :] < len_col[:, None]
    weights = jnp.where(live, jnp.float32(1.0), jnp.float32(0.0)) / len_col[:, None].astype(jnp.float32)
    values = grad_cols[:, None, :] * weights[:, :, None]
    empty = jnp.zeros((row_count, grad_cols.shape[1]), jnp.float32)
    return empty.at[id_cols.reshape(-1)].add(values.reshape(-1, grad_cols.shape[1]))


def reference(tables, feature_ids, bag_lengths, reduce_weight, expand_weight, cross_bias, cotangent):
    ids_t = jnp.transpose(feature_ids, (1, 0, 2))
    lens_t = bag_lengths.T
    pooled = lax.map(lambda a: pool_table(a[0], a[1], a[2]), (tables, ids_t, lens_t))
    pooled = jnp.transpose(pooled, (1, 0, 2)).reshape(SAMPLES, FEATURES).astype(jnp.bfloat16)
    blocks = SAMPLES // GROUP

    def step(carry, item):
        acc_reduce, acc_expand, acc_bias = carry
        block_x, block_g = item
        low = jnp.dot(block_x, reduce_weight, preferred_element_type=jnp.float32).astype(jnp.bfloat16)
        inner = jnp.dot(low, expand_weight.T, preferred_element_type=jnp.float32) + cross_bias[None, :]
        xf = block_x.astype(jnp.float32)
        crossed = (xf * inner + xf).astype(jnp.bfloat16)
        gf = block_g.astype(jnp.float32)
        grad_inner = gf * xf
        grad_inner_b = grad_inner.astype(jnp.bfloat16)
        grad_low = jnp.dot(grad_inner_b, expand_weight, preferred_element_type=jnp.float32).astype(jnp.bfloat16)
        grad_pooled = gf * (inner + 1.0) + jnp.dot(grad_low, reduce_weight.T, preferred_element_type=jnp.float32)
        acc_expand = acc_expand + jnp.dot(grad_inner_b.T, low, preferred_element_type=jnp.float32)
        acc_reduce = acc_reduce + jnp.dot(block_x.T, grad_low, preferred_element_type=jnp.float32)
        acc_bias = acc_bias + jnp.sum(grad_inner, axis=0)
        return (acc_reduce, acc_expand, acc_bias), (crossed, grad_pooled)

    zeros_w = jnp.zeros((FEATURES, RANK), jnp.float32)
    init = (zeros_w, zeros_w, jnp.zeros((FEATURES,), jnp.float32))
    items = (pooled.reshape(blocks, GROUP, FEATURES), cotangent.reshape(blocks, GROUP, FEATURES))
    (grad_reduce, grad_expand, grad_bias), (crossed, grad_pooled) = lax.scan(step, init, items)
    crossed = crossed.reshape(SAMPLES, FEATURES)
    grad_cols = jnp.transpose(grad_pooled.reshape(SAMPLES, TABLES, EMB), (1, 0, 2))
    grad_tables = lax.map(lambda a: spread_table(a[0], a[1], a[2], ROWS), (grad_cols, ids_t, lens_t))
    return crossed, grad_reduce, grad_expand, grad_bias, grad_tables
```

```python
import jax
import jax.numpy as jnp
from jax import lax
from jax.experimental import pallas as pl
from jax.experimental.pallas import tpu as pltpu
from jax.sharding import PartitionSpec as P

NX, NZH, NCORE = 8, 2, 2
NY, NZL = 8, 4
NREP = NY * NZL
TABLES, ROWS, EMB, HOT = 8, 512, 128, 4
FEATURES, RANK = TABLES * EMB, 256
GROUP = 768
HALF = GROUP // NCORE
CHUNK = HALF // NX
PIECES = 4
TPP = 4
WIDE = 64
TALL = 80
MESH = pl.DeviceIdType.MESH
BF16 = jnp.bfloat16
F32 = jnp.float32


def hops(part, way, n):
    far = n // 2
    return far if part % 2 == way else n - 1 - far


def dot(a, b, dims):
    return lax.dot_general(a, b, (dims, ((), ())), preferred_element_type=F32)


class Links:
    def __init__(self, send_sems, recv_sems):
        self.send_sems, self.recv_sems = send_sems, recv_sems
        self.used = 0
        self.sent = []

    def copy(self, src, dst, device):
        i = self.used
        self.used += 1
        made = pltpu.make_async_remote_copy(
            src_ref=src,
            dst_ref=dst,
            send_sem=self.send_sems.at[i],
            recv_sem=self.recv_sems.at[i],
            device_id=device,
            device_id_type=MESH,
        )
        made.start()
        self.sent.append(made)
        return made


COPIES = 1 + 14 + 2 + 14 + 16 + 7 * PIECES + 3 * PIECES


def kernel(
    ids_ref, lens_ref, tables_ref, rw_ref, ew_ref, bias_ref, cot_ref,
    crossed_ref, reduce_ref, expand_ref, gbias_ref, gtables_ref,
    counts, tabs_t, pooled, pooled_t, gb, gb_t, spread, inv_col, inv_row, biases,
    core_send, core_recv, rank_own, rank_send, rank_recv, zh_send, zh_recv, low,
    own_a, own_b, own_c, own_d, send_a, send_bcd, recv_a, recv_bcd, zl_send_a, zl_send, zl_recv_a, zl_recv,
    send_sems, recv_sems,
):
    m, r = lax.axis_index("mp"), lax.axis_index("replica")
    core, zh, x = lax.rem(m, 2), lax.rem(m // 2, 2), m // 4
    y, zl = r // NZL, lax.rem(r, NZL)

    def mp_at(xx, zz, cc):
        return {"mp": (xx * NZH + zz) * NCORE + cc}

    def rep_at(yy, zz):
        return {"replica": yy * NZL + zz}

    x_side = (mp_at(lax.rem(x + 1, NX), zh, core), mp_at(lax.rem(x + NX - 1, NX), zh, core))
    y_side = (rep_at(lax.rem(y + 1, NY), zl), rep_at(lax.rem(y + NY - 1, NY), zl))
    other_core, other_zh = mp_at(x, zh, 1 - core), mp_at(x, 1 - zh, core)
    zl_peer = [rep_at(y, lax.rem(zl + o, NZL)) for o in range(1, NZL)]

    barrier = pltpu.get_barrier_semaphore()
    greeted = [*x_side, *y_side, other_core, other_zh, *zl_peer]
    for device in greeted:
        pl.semaphore_signal(barrier, inc=1, device_id=device, device_id_type=MESH)

    links = Links(send_sems, recv_sems)

    inv_row[...] = 1.0 / lens_ref[...].astype(F32)
    inv_col[...] = jnp.transpose(inv_row[...])
    biases[...] = jnp.zeros_like(biases)

    def make_tab(t, carry):
        tabs_t[t] = jnp.transpose(tables_ref[t])
        return carry

    lax.fori_loop(0, TABLES, make_tab, 0)

    def half(start):
        span = pl.ds(pl.multiple_of(start, 128), HALF)
        row_of = lax.broadcasted_iota(jnp.int32, (64, HALF), 0)

        def table(t, carry):
            lens = lens_ref[pl.ds(t, 1), span]
            picks = []
            for j in range(HOT):
                picks.append(jnp.where(lens > j, ids_ref[t, j : j + 1, span], -1))
            for c in range(ROWS // 64):
                total = jnp.zeros((64, HALF), F32)
                for j in range(HOT):
                    total = jnp.where(row_of == picks[j] - 64 * c, total + 1.0, total)
                counts[t, 64 * c : 64 * c + 64, span] = total.astype(BF16)
            columns = pl.ds(pl.multiple_of(t * EMB, EMB), EMB)
            sums = dot(tabs_t[t], counts[t, :, span], ((1,), (0,)))
            mean_t = (sums * inv_row[pl.ds(t, 1), span]).astype(BF16)
            pooled_t[columns, span] = mean_t
            mean = jnp.transpose(mean_t)
            pooled[pl.ds(start, HALF), columns] = mean
            grad = cot_ref[pl.ds(start, HALF), columns].astype(F32) * mean.astype(F32)
            gb[pl.ds(start, HALF), columns] = grad.astype(BF16)
            biases[pl.ds(t, 1), :] += jnp.sum(grad, axis=0, keepdims=True)
            return carry

        lax.fori_loop(0, TABLES, table, 0)
        rows = pl.ds(start, HALF)
        return (
            dot(pooled[rows, :], rw_ref[...], ((1,), (0,))),
            dot(gb[rows, :], ew_ref[...], ((1,), (0,))),
        )

    theirs = pl.multiple_of((1 - core) * HALF, HALF)
    mine = pl.multiple_of(core * HALF, HALF)
    parts = half(theirs)
    core_send[0] = parts[0]
    core_send[1] = parts[1]
    pl.semaphore_wait(barrier, len(greeted))
    from_core = links.copy(core_send, core_recv, other_core)
    parts = half(mine)
    from_core.wait_recv()
    for p in range(2):
        rank_own[p] = (parts[p] + core_recv[p]).reshape(NX, CHUNK, RANK)

    def reduce_chain(part, n, me, own, send, recv, sides):
        count = [hops(part, way, n) for way in range(2)]
        flights = [[], []]
        for step in range(max(count)):
            for way in range(2):
                if step >= count[way]:
                    continue
                d = count[way] - step
                dest = lax.rem(me + d, n) if way == 0 else lax.rem(me + n - d, n)
                value = own(dest)
                if step > 0:
                    flights[way][step - 1].wait_recv()
                    value = value + recv(way, step - 1)[...].astype(F32)
                send(way, step)[...] = value.astype(BF16)
                flights[way].append(links.copy(send(way, step), recv(way, step), sides[way]))
            yield
        for way in range(2):
            flights[way][-1].wait_recv()
        yield [recv(way, count[way] - 1) for way in range(2)]

    rank_chains = [
        reduce_chain(
            p, NX, x,
            lambda dest, p=p: rank_own[p, dest],
            lambda way, step, p=p: rank_send.at[p, way, step],
            lambda way, step, p=p: rank_recv.at[p, way, step],
            x_side,
        )
        for p in range(2)
    ]

    def flip(t):
        gb_t[t * EMB : (t + 1) * EMB, :] = jnp.transpose(gb[:, t * EMB : (t + 1) * EMB])

    for step in range(NX // 2):
        for p in range(2):
            next(rank_chains[p])
        flip(2 * step)
        flip(2 * step + 1)

    summed = []
    swaps = []
    for p in range(2):
        arrived = next(rank_chains[p])
        value = rank_own[p, x] + arrived[0][...].astype(F32) + arrived[1][...].astype(F32)
        summed.append(value)
        zh_send[p] = value.astype(BF16)
        swaps.append(links.copy(zh_send.at[p], zh_recv.at[p], other_zh))

    def block(p, xx):
        return low.at[p, pl.ds(pl.multiple_of(mine + xx * CHUNK, 16), CHUNK), :]

    handed = [[], []]
    gathers = [[[], []], [[], []]]
    for p in range(2):
        swaps[p].wait_recv()
        block(p, x)[...] = (summed[p] + zh_recv[p].astype(F32)).astype(BF16)
        for way in range(2):
            gathers[p][way].append(links.copy(block(p, x), block(p, x), x_side[way]))
        handed[p].append(links.copy(block(p, x), block(p, x), other_core))
    for step in range(1, NX // 2 + 1):
        for p in range(2):
            for way in range(2):
                count = hops(p, way, NX)
                if step > count:
                    continue
                source = lax.rem(x + NX - step, NX) if way == 0 else lax.rem(x + step, NX)
                gathers[p][way][step - 1].wait_recv()
                if step < count:
                    gathers[p][way].append(
                        links.copy(block(p, source), block(p, source), x_side[way])
                    )
                handed[p].append(links.copy(block(p, source), block(p, source), other_core))

    owns = [own_a, own_b, own_c, own_d]

    def weight_piece(p, left, right):
        for i in range(TABLES // 2):
            value = dot(left[256 * i : 256 * i + 256, :], right, ((1,), (0,)))
            value = value.reshape(8, 32, RANK)
            owns[p][8 * i : 8 * i + 8, 0:32, :] = value[:, :, 0:128]
            owns[p][8 * i : 8 * i + 8, 32:64, :] = value[:, :, 128:256]

    def piece_chain(p):
        if p == 0:
            send = lambda way, step: send_a.at[way, step]
            recv = lambda way, step: recv_a.at[way, step]
        else:
            send = lambda way, step: send_bcd.at[p - 1, way, step]
            recv = lambda way, step: recv_bcd.at[p - 1, way, step]
        return reduce_chain(
            p, NY, y, lambda dest: owns[p][pl.ds(dest * NZL, NZL)], send, recv, y_side
        )

    last = [None] * PIECES
    spreads = [[] for _ in range(PIECES)]

    def zl_stage(p, arrived):
        def value(where):
            return (
                owns[p][y * NZL + where]
                + arrived[0][where].astype(F32)
                + arrived[1][where].astype(F32)
            )

        for o in range(1, NZL):
            out = zl_send_a.at[o - 1] if p == 0 else zl_send.at[p - 1, o - 1]
            into = zl_recv_a.at[o - 1] if p == 0 else zl_recv.at[p - 1, o - 1]
            out[...] = value(lax.rem(zl + o, NZL)).astype(BF16)
            spreads[p].append((links.copy(out, into, zl_peer[o - 1]), into))
        last[p] = value(zl)

    def finish(p):
        total = last[p]
        for copy, into in spreads[p]:
            copy.wait_recv()
            total = total + into[...].astype(F32)
        if p < 2:
            out = (expand_ref, reduce_ref)[p]
            out[:, 0:128] = total[0:32, :]
            out[:, 128:256] = total[32:64, :]
            if p == 0:
                line = total[64:65, :]
                picked = line[:, 0:32]
                for k in range(1, NZL):
                    picked = jnp.where(zl == k, line[:, 32 * k : 32 * k + 32], picked)
                gbias_ref[...] = picked
        else:
            for t in range(TPP):
                gtables_ref[(p - 2) * TPP + t] = total[16 * t : 16 * t + 16, :]

    for copy in handed[0]:
        copy.wait_recv()
    for t in range(TABLES):
        own_a[NZL * t : NZL * t + NZL, 64:80, :] = jnp.broadcast_to(
            biases[t : t + 1, :].reshape(1, 1, EMB), (NZL, 16, EMB)
        )
    weight_piece(0, gb_t, low[0])
    chains = [piece_chain(p) for p in range(PIECES)]
    next(chains[0])

    for copy in handed[1]:
        copy.wait_recv()
    weight_piece(1, pooled_t, low[1])
    next(chains[1])
    next(chains[0])

    def cross(i):
        pair = slice(256 * i, 256 * i + 256)
        for c in range(GROUP // 256):
            rows = slice(256 * c, 256 * c + 256)
            inner2 = dot(low[0, rows, :], ew_ref[pair, :], ((1,), (1,)))
            back2 = dot(low[1, rows, :], rw_ref[pair, :], ((1,), (1,)))
            for u in range(2):
                t = 2 * i + u
                columns = slice(t * EMB, (t + 1) * EMB)
                inner = inner2[:, u * EMB : (u + 1) * EMB] + bias_ref[t : t + 1, :]
                xf = pooled[rows, columns].astype(F32)
                crossed_ref[rows, columns] = (xf * inner + xf).astype(BF16)
                gf = cot_ref[rows, columns].astype(F32)
                grad = gf * (inner + 1.0) + back2[:, u * EMB : (u + 1) * EMB]
                spread[rows, columns] = (grad * inv_col[rows, t : t + 1]).astype(BF16)

    def table_piece(p):
        for k in range(TPP):
            t = (p - 2) * TPP + k
            value = dot(counts[t], spread[:, t * EMB : (t + 1) * EMB], ((1,), (0,)))
            owns[p][:, 16 * k : 16 * k + 16, :] = value.reshape(NREP, 16, EMB)

    cross(0)
    cross(1)
    next(chains[1])
    next(chains[0])
    table_piece(2)
    next(chains[2])
    next(chains[1])
    next(chains[0])
    cross(2)
    cross(3)
    next(chains[2])
    next(chains[1])
    table_piece(3)
    next(chains[3])
    next(chains[2])
    zl_stage(0, next(chains[0]))
    next(chains[3])
    next(chains[2])
    zl_stage(1, next(chains[1]))
    next(chains[3])
    finish(0)
    zl_stage(2, next(chains[2]))
    next(chains[3])
    finish(1)
    zl_stage(3, next(chains[3]))
    finish(2)
    finish(3)
    for copy in links.sent:
        copy.wait_send()


def body(tables, feature_ids, bag_lengths, reduce_weight, expand_weight, cross_bias, cotangent):
    vmem = pl.BlockSpec(memory_space=pltpu.VMEM)
    crossed, grad_reduce, grad_expand, grad_bias, grad_tables = pl.pallas_call(
        kernel,
        out_shape=(
            jax.ShapeDtypeStruct((GROUP, FEATURES), BF16),
            jax.ShapeDtypeStruct((FEATURES // NREP, RANK), F32),
            jax.ShapeDtypeStruct((FEATURES // NREP, RANK), F32),
            jax.ShapeDtypeStruct((1, FEATURES // NREP), F32),
            jax.ShapeDtypeStruct((TABLES, ROWS // NREP, EMB), F32),
        ),
        in_specs=[vmem] * 7,
        out_specs=(vmem,) * 5,
        scratch_shapes=[
            pltpu.VMEM((TABLES, ROWS, GROUP), BF16),
            pltpu.VMEM((TABLES, EMB, ROWS), BF16),
            pltpu.VMEM((GROUP, FEATURES), BF16),
            pltpu.VMEM((FEATURES, GROUP), BF16),
            pltpu.VMEM((GROUP, FEATURES), BF16),
            pltpu.VMEM((FEATURES, GROUP), BF16),
            pltpu.VMEM((GROUP, FEATURES), BF16),
            pltpu.VMEM((GROUP, TABLES), F32),
            pltpu.VMEM((TABLES, GROUP), F32),
            pltpu.VMEM((TABLES, EMB), F32),
            pltpu.VMEM((2, HALF, RANK), F32),
            pltpu.VMEM((2, HALF, RANK), F32),
            pltpu.VMEM((2, NX, CHUNK, RANK), F32),
            pltpu.VMEM((2, 2, NX // 2, CHUNK, RANK), BF16),
            pltpu.VMEM((2, 2, NX // 2, CHUNK, RANK), BF16),
            pltpu.VMEM((2, CHUNK, RANK), BF16),
            pltpu.VMEM((2, CHUNK, RANK), BF16),
            pltpu.VMEM((2, GROUP, RANK), BF16),
            pltpu.VMEM((NREP, TALL, EMB), F32),
            pltpu.VMEM((NREP, WIDE, EMB), F32),
            pltpu.VMEM((NREP, WIDE, EMB), F32),
            pltpu.VMEM((NREP, WIDE, EMB), F32),
            pltpu.VMEM((2, NY // 2, NZL, TALL, EMB), BF16),
            pltpu.VMEM((PIECES - 1, 2, NY // 2, NZL, WIDE, EMB), BF16),
            pltpu.VMEM((2, NY // 2, NZL, TALL, EMB), BF16),
            pltpu.VMEM((PIECES - 1, 2, NY // 2, NZL, WIDE, EMB), BF16),
            pltpu.VMEM((NZL - 1, TALL, EMB), BF16),
            pltpu.VMEM((PIECES - 1, NZL - 1, WIDE, EMB), BF16),
            pltpu.VMEM((NZL - 1, TALL, EMB), BF16),
            pltpu.VMEM((PIECES - 1, NZL - 1, WIDE, EMB), BF16),
            pltpu.SemaphoreType.DMA((COPIES,)),
            pltpu.SemaphoreType.DMA((COPIES,)),
        ],
        compiler_params=pltpu.CompilerParams(
            collective_id=0, has_side_effects=True, vmem_limit_bytes=56 << 20
        ),
        cost_estimate=pl.CostEstimate(
            flops=5 << 30, bytes_accessed=8 << 20, transcendentals=0
        ),
    )(
        jnp.transpose(feature_ids, (1, 2, 0)),
        bag_lengths.T,
        tables,
        reduce_weight,
        expand_weight,
        cross_bias.reshape(TABLES, EMB),
        cotangent,
    )
    return crossed, grad_reduce, grad_expand, grad_bias.reshape(-1), grad_tables


def solution(mesh):
    in_specs = (
        P("mp", None, None),
        P("replica", "mp", None),
        P("replica", "mp"),
        P("mp", None),
        P("mp", None),
        P("mp"),
        P("replica", "mp"),
    )
    out_specs = (
        P("replica", "mp"),
        P(("mp", "replica"), None),
        P(("mp", "replica"), None),
        P(("mp", "replica")),
        P("mp", "replica", None),
    )
    return jax.shard_map(body, mesh=mesh, in_specs=in_specs, out_specs=out_specs, check_vma=False)
```

```python
import jax
import jax.numpy as jnp
from jax import lax
from jax.experimental import pallas as pl
from jax.experimental.pallas import tpu as pltpu
from jax.sharding import PartitionSpec as P

NX, NZH, NCORE = 8, 2, 2
NY, NZL = 8, 4
NREP = NY * NZL
TABLES, ROWS, EMB, HOT = 8, 512, 128, 4
FEATURES, RANK = TABLES * EMB, 256
GROUP = 768
HALF = GROUP // NCORE
CHUNK = HALF // NX
PIECES = 4
TPP = 4
WIDE = 64
TALL = 80
FAR_FIRST = (4, 3, 5, 2, 6, 1, 7)
MESH = pl.DeviceIdType.MESH
BF16 = jnp.bfloat16
F32 = jnp.float32


def hops(part, way, n):
    far = n // 2
    return far if part % 2 == way else n - 1 - far


def dot(a, b, dims):
    return lax.dot_general(a, b, (dims, ((), ())), preferred_element_type=F32)


class Links:
    def __init__(self, send_sems, recv_sems):
        self.send_sems, self.recv_sems = send_sems, recv_sems
        self.used = 0
        self.sent = []

    def copy(self, src, dst, device):
        i = self.used
        self.used += 1
        made = pltpu.make_async_remote_copy(
            src_ref=src,
            dst_ref=dst,
            send_sem=self.send_sems.at[i],
            recv_sem=self.recv_sems.at[i],
            device_id=device,
            device_id_type=MESH,
        )
        made.start()
        self.sent.append(made)
        return made


COPIES = 1 + 14 + 2 + 14 + 16 + 7 * PIECES + 3 * PIECES


def kernel(
    ids_hbm, lens_hbm, tables_hbm, cot_hbm, rw_hbm, ew_hbm, bias_hbm,
    crossed_ref, reduce_ref, expand_ref, gbias_ref, gtables_ref,
    ids_ref, lens_ref, tables_ref, cot_ref, rw_ref, ew_ref, bias_ref, load_sems,
    counts, tabs_t, pooled, pooled_t, gb, gb_t, spread, inv_col, inv_row, biases,
    core_send, core_recv, rank_own, rank_send, rank_recv, zh_send, zh_recv, low,
    own_a, own_b, own_c, own_d, near_send, near_recv, across_send, across_recv,
    send_a, send_bcd, recv_a, recv_bcd, zl_send, zl_recv,
    send_sems, recv_sems,
):
    m, r = lax.axis_index("mp"), lax.axis_index("replica")
    core, zh, x = lax.rem(m, 2), lax.rem(m // 2, 2), m // 4
    y, zl = r // NZL, lax.rem(r, NZL)

    def mp_at(xx, zz, cc):
        return {"mp": (xx * NZH + zz) * NCORE + cc}

    def rep_at(yy, zz):
        return {"replica": yy * NZL + zz}

    x_side = (mp_at(lax.rem(x + 1, NX), zh, core), mp_at(lax.rem(x + NX - 1, NX), zh, core))
    y_side = (rep_at(lax.rem(y + 1, NY), zl), rep_at(lax.rem(y + NY - 1, NY), zl))
    other_core, other_zh = mp_at(x, zh, 1 - core), mp_at(x, 1 - zh, core)
    zl_peer = [rep_at(y, lax.rem(zl + o, NZL)) for o in range(1, NZL)]

    barrier = pltpu.get_barrier_semaphore()
    x_peer = [mp_at(lax.rem(x + o, NX), zh, core) for o in range(1, NX)]
    greeted = [*x_peer, *y_side, other_core, other_zh, *zl_peer]
    for device in greeted:
        pl.semaphore_signal(barrier, inc=1, device_id=device, device_id_type=MESH)

    inputs = (ids_hbm, lens_hbm, tables_hbm, cot_hbm, rw_hbm, ew_hbm, bias_hbm)
    places = (ids_ref, lens_ref, tables_ref, cot_ref, rw_ref, ew_ref, bias_ref)
    loads = []
    for i in range(len(inputs)):
        loads.append(pltpu.make_async_copy(inputs[i], places[i], load_sems.at[i]))
        loads[i].start()

    links = Links(send_sems, recv_sems)

    loads[0].wait()
    loads[1].wait()
    inv_row[...] = 1.0 / lens_ref[...].astype(F32)
    inv_col[...] = jnp.transpose(inv_row[...])
    biases[...] = jnp.zeros_like(biases)

    def half(start, first):
        span = pl.ds(pl.multiple_of(start, 128), HALF)
        row_of = lax.broadcasted_iota(jnp.int32, (64, HALF), 0).astype(F32).astype(BF16)
        one, zero = jnp.ones((), BF16), jnp.zeros((64, HALF), BF16)
        for t in range(TABLES):
            lens = lens_ref[t : t + 1, span]
            picks = []
            for j in range(HOT):
                picks.append(jnp.where(lens > j, ids_ref[t, j : j + 1, span], -1))
            for c in range(ROWS // 64):
                total = zero
                for j in range(HOT):
                    pick = (picks[j] - 64 * c).astype(F32).astype(BF16)
                    total = jnp.where(row_of == pick, total + one, total)
                counts[t, 64 * c : 64 * c + 64, span] = total
            if first:
                if t == 0:
                    loads[2].wait()
                    loads[3].wait()
                tabs_t[t] = jnp.transpose(tables_ref[t])
            columns = slice(t * EMB, (t + 1) * EMB)
            sums = dot(tabs_t[t], counts[t, :, span], ((1,), (0,)))
            mean_t = (sums * inv_row[t : t + 1, span]).astype(BF16)
            pooled_t[columns, span] = mean_t
            mean = jnp.transpose(mean_t)
            pooled[pl.ds(start, HALF), columns] = mean
            grad = cot_ref[pl.ds(start, HALF), columns].astype(F32) * mean.astype(F32)
            gb[pl.ds(start, HALF), columns] = grad.astype(BF16)
            biases[t : t + 1, :] += jnp.sum(grad, axis=0, keepdims=True)
        if first:
            for i in range(4, 7):
                loads[i].wait()
        rows = pl.ds(start, HALF)
        return (
            dot(pooled[rows, :], rw_ref[...], ((1,), (0,))),
            dot(gb[rows, :], ew_ref[...], ((1,), (0,))),
        )

    theirs = pl.multiple_of((1 - core) * HALF, HALF)
    mine = pl.multiple_of(core * HALF, HALF)
    parts = half(theirs, True)
    core_send[0] = parts[0]
    core_send[1] = parts[1]
    pl.semaphore_wait(barrier, len(greeted))
    from_core = links.copy(core_send, core_recv, other_core)
    parts = half(mine, False)
    from_core.wait_recv()
    for p in range(2):
        rank_own[p] = (parts[p] + core_recv[p]).reshape(NX, CHUNK, RANK)

    def reduce_chain(part, n, me, own, send, recv, sides):
        count = [hops(part, way, n) for way in range(2)]
        flights = [[], []]
        for step in range(max(count)):
            for way in range(2):
                if step >= count[way]:
                    continue
                d = count[way] - step
                dest = lax.rem(me + d, n) if way == 0 else lax.rem(me + n - d, n)
                value = own(dest)
                if step > 0:
                    flights[way][step - 1].wait_recv()
                    value = value + recv(way, step - 1)[...].astype(F32)
                send(way, step)[...] = value.astype(BF16)
                flights[way].append(links.copy(send(way, step), recv(way, step), sides[way]))
            yield
        for way in range(2):
            flights[way][-1].wait_recv()
        yield [recv(way, count[way] - 1) for way in range(2)]

    scatters = [[], []]
    for p in range(2):
        for o in FAR_FIRST:
            rank_send[p, o - 1] = rank_own[p, lax.rem(x + o, NX)].astype(BF16)
            scatters[p].append(
                links.copy(rank_send.at[p, o - 1], rank_recv.at[p, o - 1], x_peer[o - 1])
            )

    for t in range(TABLES):
        gb_t[t * EMB : (t + 1) * EMB, :] = jnp.transpose(gb[:, t * EMB : (t + 1) * EMB])

    summed = []
    swaps = []
    for p in range(2):
        value = rank_own[p, x]
        for i, o in enumerate(FAR_FIRST):
            scatters[p][i].wait_recv()
            value = value + rank_recv[p, o - 1].astype(F32)
        summed.append(value)
        zh_send[p] = value.astype(BF16)
        swaps.append(links.copy(zh_send.at[p], zh_recv.at[p], other_zh))

    def block(p, xx):
        return low.at[p, pl.ds(pl.multiple_of(mine + xx * CHUNK, 16), CHUNK), :]

    handed = [[], []]
    gathers = [[], []]
    for p in range(2):
        swaps[p].wait_recv()
        block(p, x)[...] = (summed[p] + zh_recv[p].astype(F32)).astype(BF16)
        for o in FAR_FIRST:
            gathers[p].append(links.copy(block(p, x), block(p, x), x_peer[o - 1]))
    for p in range(2):
        for copy in gathers[p]:
            copy.wait_recv()
        rows = low.at[p, pl.ds(mine, HALF), :]
        handed[p].append(links.copy(rows, rows, other_core))

    owns = [own_a, own_b, own_c, own_d]

    def weight_piece(p, left, right):
        for i in range(TABLES // 2):
            value = dot(left[256 * i : 256 * i + 256, :], right, ((1,), (0,)))
            value = value.reshape(8, 32, RANK)
            if p == 0:
                for k in range(8):
                    own_a[k % NZL, 2 * i + k // NZL, 0:32, :] = value[k, :, 0:128]
                    own_a[k % NZL, 2 * i + k // NZL, 32:64, :] = value[k, :, 128:256]
                continue
            owns[p][8 * i : 8 * i + 8, 0:32, :] = value[:, :, 0:128]
            owns[p][8 * i : 8 * i + 8, 32:64, :] = value[:, :, 128:256]

    def piece_chain(p):
        return reduce_chain(
            p, NY, y,
            lambda dest: owns[p][pl.ds(dest * NZL, NZL)],
            lambda way, step: send_bcd.at[p - 1, way, step],
            lambda way, step: recv_bcd.at[p - 1, way, step],
            y_side,
        )

    def first_chain():
        near = zl + 1 - 2 * lax.rem(zl, 2)
        across = lax.rem(zl + 2, NZL)
        firsts = []
        for k, keeper in enumerate((lax.rem(near + 2, NZL), near)):
            near_send[k] = own_a[keeper].astype(BF16)
            firsts.append(links.copy(near_send.at[k], near_recv.at[k], rep_at(y, near)))
        yield
        firsts[0].wait_recv()
        across_send[...] = (own_a[across] + near_recv[0].astype(F32)).astype(BF16)
        second = links.copy(across_send, across_recv, rep_at(y, across))
        yield
        firsts[1].wait_recv()
        second.wait_recv()
        for k in range(NY):
            own_a[zl, k] += near_recv[1, k].astype(F32) + across_recv[k].astype(F32)
        yield from reduce_chain(
            0, NY, y,
            lambda dest: own_a[zl, dest],
            lambda way, step: send_a.at[way, step],
            lambda way, step: recv_a.at[way, step],
            y_side,
        )

    last = [None] * PIECES
    spreads = [[] for _ in range(PIECES)]

    def zl_stage(p, arrived):
        def value(where):
            return (
                owns[p][y * NZL + where]
                + arrived[0][where].astype(F32)
                + arrived[1][where].astype(F32)
            )

        for o in range(1, NZL):
            out, into = zl_send.at[p - 1, o - 1], zl_recv.at[p - 1, o - 1]
            out[...] = value(lax.rem(zl + o, NZL)).astype(BF16)
            spreads[p].append((links.copy(out, into, zl_peer[o - 1]), into))
        last[p] = value(zl)

    def finish(p):
        total = last[p]
        for copy, into in spreads[p]:
            copy.wait_recv()
            total = total + into[...].astype(F32)
        if p < 2:
            out = (expand_ref, reduce_ref)[p]
            out[:, 0:128] = total[0:32, :]
            out[:, 128:256] = total[32:64, :]
            if p == 0:
                line = total[64:65, :]
                picked = line[:, 0:32]
                for k in range(1, NZL):
                    picked = jnp.where(zl == k, line[:, 32 * k : 32 * k + 32], picked)
                gbias_ref[...] = picked
        else:
            for t in range(TPP):
                gtables_ref[(p - 2) * TPP + t] = total[16 * t : 16 * t + 16, :]

    for copy in handed[0]:
        copy.wait_recv()
    for t in range(TABLES):
        own_a[:, t, 64:80, :] = jnp.broadcast_to(
            biases[t : t + 1, :].reshape(1, 1, EMB), (NZL, 16, EMB)
        )
    weight_piece(0, gb_t, low[0])
    chains = [first_chain()] + [piece_chain(p) for p in range(1, PIECES)]
    next(chains[0])

    for copy in handed[1]:
        copy.wait_recv()
    weight_piece(1, pooled_t, low[1])
    next(chains[1])

    def cross(i):
        pair = slice(256 * i, 256 * i + 256)
        for c in range(GROUP // 256):
            rows = slice(256 * c, 256 * c + 256)
            inner2 = dot(low[0, rows, :], ew_ref[pair, :], ((1,), (1,)))
            back2 = dot(low[1, rows, :], rw_ref[pair, :], ((1,), (1,)))
            for u in range(2):
                t = 2 * i + u
                columns = slice(t * EMB, (t + 1) * EMB)
                inner = inner2[:, u * EMB : (u + 1) * EMB] + bias_ref[t : t + 1, :]
                xf = pooled[rows, columns].astype(F32)
                crossed_ref[rows, columns] = (xf * inner + xf).astype(BF16)
                gf = cot_ref[rows, columns].astype(F32)
                grad = gf * (inner + 1.0) + back2[:, u * EMB : (u + 1) * EMB]
                spread[rows, columns] = (grad * inv_col[rows, t : t + 1]).astype(BF16)

    def table_piece(p):
        for k in range(TPP):
            t = (p - 2) * TPP + k
            value = dot(counts[t], spread[:, t * EMB : (t + 1) * EMB], ((1,), (0,)))
            owns[p][:, 16 * k : 16 * k + 16, :] = value.reshape(NREP, 16, EMB)

    cross(0)
    cross(1)
    next(chains[1])
    table_piece(2)
    next(chains[2])
    next(chains[1])
    next(chains[0])
    cross(2)
    cross(3)
    next(chains[2])
    next(chains[1])
    table_piece(3)
    next(chains[3])
    next(chains[2])
    next(chains[0])
    next(chains[3])
    zl_stage(1, next(chains[1]))
    next(chains[2])
    next(chains[0])
    next(chains[3])
    zl_stage(2, next(chains[2]))
    next(chains[0])
    next(chains[3])
    finish(1)
    next(chains[0])
    zl_stage(3, next(chains[3]))
    arrived = next(chains[0])
    last[0] = own_a[zl, y] + arrived[0][...].astype(F32) + arrived[1][...].astype(F32)
    finish(0)
    finish(2)
    finish(3)
    for copy in links.sent:
        copy.wait_send()


def hand_out(*refs):
    sems = refs[10]
    copies = [pltpu.make_async_copy(refs[i], refs[5 + i], sems.at[i]) for i in range(5)]
    for copy in copies:
        copy.start()
    for copy in copies:
        copy.wait()


def body(tables, feature_ids, bag_lengths, reduce_weight, expand_weight, cross_bias, cotangent):
    vmem = pl.BlockSpec(memory_space=pltpu.VMEM)
    anywhere = pl.BlockSpec(memory_space=pl.ANY)
    kept = (
        ((GROUP, FEATURES), BF16),
        ((FEATURES // NREP, RANK), F32),
        ((FEATURES // NREP, RANK), F32),
        ((1, FEATURES // NREP), F32),
        ((TABLES, ROWS // NREP, EMB), F32),
    )
    made = pl.pallas_call(
        kernel,
        out_shape=tuple(pltpu.VMEM(*k) for k in kept),
        in_specs=[pl.BlockSpec(memory_space=pltpu.HBM)] * 7,
        out_specs=(vmem,) * 5,
        scratch_shapes=[
            pltpu.VMEM((TABLES, HOT, GROUP), jnp.int32),
            pltpu.VMEM((TABLES, GROUP), jnp.int32),
            pltpu.VMEM((TABLES, ROWS, EMB), BF16),
            pltpu.VMEM((GROUP, FEATURES), BF16),
            pltpu.VMEM((FEATURES, RANK), BF16),
            pltpu.VMEM((FEATURES, RANK), BF16),
            pltpu.VMEM((TABLES, EMB), F32),
            pltpu.SemaphoreType.DMA((7,)),
            pltpu.VMEM((TABLES, ROWS, GROUP), BF16),
            pltpu.VMEM((TABLES, EMB, ROWS), BF16),
            pltpu.VMEM((GROUP, FEATURES), BF16),
            pltpu.VMEM((FEATURES, GROUP), BF16),
            pltpu.VMEM((GROUP, FEATURES), BF16),
            pltpu.VMEM((FEATURES, GROUP), BF16),
            pltpu.VMEM((GROUP, FEATURES), BF16),
            pltpu.VMEM((GROUP, TABLES), F32),
            pltpu.VMEM((TABLES, GROUP), F32),
            pltpu.VMEM((TABLES, EMB), F32),
            pltpu.VMEM((2, HALF, RANK), F32),
            pltpu.VMEM((2, HALF, RANK), F32),
            pltpu.VMEM((2, NX, CHUNK, RANK), F32),
            pltpu.VMEM((2, NX - 1, CHUNK, RANK), BF16),
            pltpu.VMEM((2, NX - 1, CHUNK, RANK), BF16),
            pltpu.VMEM((2, CHUNK, RANK), BF16),
            pltpu.VMEM((2, CHUNK, RANK), BF16),
            pltpu.VMEM((2, GROUP, RANK), BF16),
            pltpu.VMEM((NZL, NY, TALL, EMB), F32),
            pltpu.VMEM((NREP, WIDE, EMB), F32),
            pltpu.VMEM((NREP, WIDE, EMB), F32),
            pltpu.VMEM((NREP, WIDE, EMB), F32),
            pltpu.VMEM((2, NY, TALL, EMB), BF16),
            pltpu.VMEM((2, NY, TALL, EMB), BF16),
            pltpu.VMEM((NY, TALL, EMB), BF16),
            pltpu.VMEM((NY, TALL, EMB), BF16),
            pltpu.VMEM((2, NY // 2, TALL, EMB), BF16),
            pltpu.VMEM((PIECES - 1, 2, NY // 2, NZL, WIDE, EMB), BF16),
            pltpu.VMEM((2, NY // 2, TALL, EMB), BF16),
            pltpu.VMEM((PIECES - 1, 2, NY // 2, NZL, WIDE, EMB), BF16),
            pltpu.VMEM((PIECES - 1, NZL - 1, WIDE, EMB), BF16),
            pltpu.VMEM((PIECES - 1, NZL - 1, WIDE, EMB), BF16),
            pltpu.SemaphoreType.DMA((COPIES,)),
            pltpu.SemaphoreType.DMA((COPIES,)),
        ],
        compiler_params=pltpu.CompilerParams(
            collective_id=0, has_side_effects=True, vmem_limit_bytes=62 << 20
        ),
        cost_estimate=pl.CostEstimate(
            flops=5 << 30, bytes_accessed=8 << 20, transcendentals=0
        ),
    )(
        jnp.transpose(feature_ids, (1, 2, 0)),
        bag_lengths.T,
        tables,
        cotangent,
        reduce_weight,
        expand_weight,
        cross_bias.reshape(TABLES, EMB),
    )
    crossed, grad_reduce, grad_expand, grad_bias, grad_tables = made
    return crossed, grad_reduce, grad_expand, grad_bias.reshape(-1), grad_tables


def solution(mesh):
    in_specs = (
        P("mp", None, None),
        P("replica", "mp", None),
        P("replica", "mp"),
        P("mp", None),
        P("mp", None),
        P("mp"),
        P("replica", "mp"),
    )
    out_specs = (
        P("replica", "mp"),
        P(("mp", "replica"), None),
        P(("mp", "replica"), None),
        P(("mp", "replica")),
        P("mp", "replica", None),
    )
    return jax.shard_map(body, mesh=mesh, in_specs=in_specs, out_specs=out_specs, check_vma=False)
```

```python
import jax
import jax.numpy as jnp
from jax import lax
from jax.experimental import pallas as pl
from jax.experimental.pallas import tpu as pltpu
from jax.sharding import PartitionSpec as P

NX, NZH, NCORE = 8, 2, 2
NY, NZL = 8, 4
NREP = NY * NZL
TABLES, ROWS, EMB, HOT = 8, 512, 128, 4
FEATURES, RANK = TABLES * EMB, 256
GROUP = 768
HALF = GROUP // NCORE
CHUNK = HALF // NX
PIECES = 4
TPP = 4
WIDE = 64
TALL = 80
MESH = pl.DeviceIdType.MESH
BF16 = jnp.bfloat16
F32 = jnp.float32


def hops(part, way, n):
    far = n // 2
    return far if part % 2 == way else n - 1 - far


def dot(a, b, dims):
    return lax.dot_general(a, b, (dims, ((), ())), preferred_element_type=F32)


class Links:
    def __init__(self, send_sems, recv_sems):
        self.send_sems, self.recv_sems = send_sems, recv_sems
        self.used = 0
        self.sent = []

    def copy(self, src, dst, device):
        i = self.used
        self.used += 1
        made = pltpu.make_async_remote_copy(
            src_ref=src,
            dst_ref=dst,
            send_sem=self.send_sems.at[i],
            recv_sem=self.recv_sems.at[i],
            device_id=device,
            device_id_type=MESH,
        )
        made.start()
        self.sent.append(made)
        return made


COPIES = 2 + 14 + 2 + 14 + 2 + 3 + 7 * PIECES + 3 * (PIECES - 1)


def kernel(
    ids_hbm, lens_hbm, tables_hbm, cot_hbm, rw_hbm, ew_hbm, bias_hbm,
    crossed_ref, reduce_ref, expand_ref, gbias_ref, gtables_ref,
    ids_ref, lens_ref, tables_ref, cot_ref, rw_ref, ew_ref, bias_ref, load_sems,
    counts, tabs_t, pooled, pooled_t, gb, gb_t, spread, inv_col, inv_row, biases,
    core_send, core_recv, rank_own, rank_send, rank_recv, zh_send, zh_recv, low,
    own_a, own_b, own_c, own_d, near_send, near_recv, across_send, across_recv,
    send_a, send_bcd, recv_a, recv_bcd, zl_send, zl_recv,
    send_sems, recv_sems,
):
    m, r = lax.axis_index("mp"), lax.axis_index("replica")
    core, zh, x = lax.rem(m, 2), lax.rem(m // 2, 2), m // 4
    y, zl = r // NZL, lax.rem(r, NZL)

    def mp_at(xx, zz, cc):
        return {"mp": (xx * NZH + zz) * NCORE + cc}

    def rep_at(yy, zz):
        return {"replica": yy * NZL + zz}

    y_side = (rep_at(lax.rem(y + 1, NY), zl), rep_at(lax.rem(y + NY - 1, NY), zl))
    other_core, other_zh = mp_at(x, zh, 1 - core), mp_at(x, 1 - zh, core)
    zl_peer = [rep_at(y, lax.rem(zl + o, NZL)) for o in range(1, NZL)]

    x_at = [
        [x] + [lax.rem(x + o, NX) for o in range(1, 5)],
        [x] + [lax.rem(x + NX - o, NX) for o in range(1, 5)],
    ]
    x_dev = [[None] + [mp_at(x_at[way][o], zh, core) for o in (1, 2)] for way in range(2)]

    barrier = pltpu.get_barrier_semaphore()
    greeted = [*x_dev[0][1:], *x_dev[1][1:], *y_side, other_core, other_zh, *zl_peer]
    for device in greeted:
        pl.semaphore_signal(barrier, inc=1, device_id=device, device_id_type=MESH)

    inputs = (ids_hbm, lens_hbm, tables_hbm, cot_hbm, rw_hbm, ew_hbm, bias_hbm)
    places = (ids_ref, lens_ref, tables_ref, cot_ref, rw_ref, ew_ref, bias_ref)
    loads = []
    for i in range(len(inputs)):
        loads.append(pltpu.make_async_copy(inputs[i], places[i], load_sems.at[i]))
        loads[i].start()

    links = Links(send_sems, recv_sems)

    loads[0].wait()
    loads[1].wait()
    inv_row[...] = 1.0 / lens_ref[...].astype(F32)
    inv_col[...] = jnp.transpose(inv_row[...])
    biases[...] = jnp.zeros_like(biases)

    def half(start, first):
        span = pl.ds(pl.multiple_of(start, 128), HALF)
        row_of = lax.broadcasted_iota(jnp.int32, (64, HALF), 0).astype(F32).astype(BF16)
        one, zero = jnp.ones((), BF16), jnp.zeros((64, HALF), BF16)
        for t in range(TABLES):
            lens = lens_ref[t : t + 1, span]
            picks = []
            for j in range(HOT):
                picks.append(jnp.where(lens > j, ids_ref[t, j : j + 1, span], -1))
            for c in range(ROWS // 64):
                total = zero
                for j in range(HOT):
                    pick = (picks[j] - 64 * c).astype(F32).astype(BF16)
                    total = jnp.where(row_of == pick, total + one, total)
                counts[t, 64 * c : 64 * c + 64, span] = total
            if first:
                if t == 0:
                    loads[2].wait()
                    loads[3].wait()
                tabs_t[t] = jnp.transpose(tables_ref[t])
            columns = slice(t * EMB, (t + 1) * EMB)
            sums = dot(tabs_t[t], counts[t, :, span], ((1,), (0,)))
            mean_t = (sums * inv_row[t : t + 1, span]).astype(BF16)
            pooled_t[columns, span] = mean_t
            mean = jnp.transpose(mean_t)
            pooled[pl.ds(start, HALF), columns] = mean
            grad = cot_ref[pl.ds(start, HALF), columns].astype(F32) * mean.astype(F32)
            gb[pl.ds(start, HALF), columns] = grad.astype(BF16)
            biases[t : t + 1, :] += jnp.sum(grad, axis=0, keepdims=True)
        if first:
            for i in range(4, 7):
                loads[i].wait()
        rows = pl.ds(start, HALF)
        return (
            dot(pooled[rows, :], rw_ref[...], ((1,), (0,))),
            dot(gb[rows, :], ew_ref[...], ((1,), (0,))),
        )

    theirs = pl.multiple_of((1 - core) * HALF, HALF)
    mine = pl.multiple_of(core * HALF, HALF)
    parts = half(theirs, True)
    for p in range(2):
        core_send[p] = parts[p].astype(BF16)
    pl.semaphore_wait(barrier, len(greeted))
    from_core = [
        links.copy(core_send.at[p], core_recv.at[p], other_core) for p in range(2)
    ]
    parts = half(mine, False)

    scatters = [{}, {}]
    gathers = [{}, {}]
    swaps = [None, None]
    summed = [None, None]
    handed = [None, None]

    def scatter(p, way, d, value, to):
        rank_send[p, way, d - 1] = value.astype(BF16)
        scatters[p][way, d] = links.copy(
            rank_send.at[p, way, d - 1], rank_recv.at[p, way, d - 1], x_dev[way][to]
        )

    def arrived(p, way, d):
        scatters[p][way, d].wait_recv()
        return rank_recv[p, way, d - 1].astype(F32)

    def scatter_first(p):
        from_core[p].wait_recv()
        rank_own[p] = (parts[p] + core_recv[p].astype(F32)).reshape(NX, CHUNK, RANK)
        for way in range(2):
            if hops(p, way, NX) == 4:
                scatter(p, way, 4, rank_own[p, x_at[way][4]], 2)
        for way in range(2):
            scatter(p, way, 3, rank_own[p, x_at[way][3]], 1)
        for way in range(2):
            scatter(p, way, 1, rank_own[p, x_at[way][1]], 1)

    def scatter_second(p):
        for way in range(2):
            value = rank_own[p, x_at[way][2]] + arrived(p, way, 3)
            if hops(p, way, NX) == 4:
                value = value + arrived(p, way, 4)
            scatter(p, way, 2, value, 2)

    def scatter_last(p):
        value = rank_own[p, x]
        for d in (1, 2):
            for way in range(2):
                value = value + arrived(p, way, d)
        summed[p] = value
        zh_send[p] = value.astype(BF16)
        swaps[p] = links.copy(zh_send.at[p], zh_recv.at[p], other_zh)

    def block(p, xx):
        return low.at[p, pl.ds(pl.multiple_of(mine + xx * CHUNK, 16), CHUNK), :]

    def gather_first(p):
        swaps[p].wait_recv()
        block(p, x)[...] = (summed[p] + zh_recv[p].astype(F32)).astype(BF16)
        for d in (2, 1):
            for way in range(2):
                gathers[p][way, d] = links.copy(block(p, x), block(p, x), x_dev[way][d])

    def gather_second(p):
        for way in range(2):
            source = block(p, x_at[1 - way][2])
            gathers[p][way, 2].wait_recv()
            for d in range(3, hops(p, way, NX) + 1):
                gathers[p][way, d] = links.copy(source, source, x_dev[way][d - 2])

    def gather_last(p):
        for (way, d), copy in gathers[p].items():
            if d != 2:
                copy.wait_recv()
        rows = low.at[p, pl.ds(mine, HALF), :]
        handed[p] = links.copy(rows, rows, other_core)

    def flip(t):
        gb_t[t * EMB : (t + 1) * EMB, :] = jnp.transpose(gb[:, t * EMB : (t + 1) * EMB])

    scatter_first(0)
    scatter_first(1)
    for t in range(TABLES // 2):
        flip(t)
    scatter_second(0)
    scatter_second(1)
    for t in range(TABLES // 2, TABLES):
        flip(t)
    scatter_last(0)
    scatter_last(1)
    gather_first(0)
    gather_first(1)
    gather_second(0)
    gather_second(1)
    gather_last(0)
    gather_last(1)

    def reduce_chain(part, n, me, own, send, recv, sides):
        count = [hops(part, way, n) for way in range(2)]
        flights = [[], []]
        for step in range(max(count)):
            for way in range(2):
                if step >= count[way]:
                    continue
                d = count[way] - step
                dest = lax.rem(me + d, n) if way == 0 else lax.rem(me + n - d, n)
                value = own(dest)
                if step > 0:
                    flights[way][step - 1].wait_recv()
                    value = value + recv(way, step - 1)[...].astype(F32)
                send(way, step)[...] = value.astype(BF16)
                flights[way].append(links.copy(send(way, step), recv(way, step), sides[way]))
            yield
        for way in range(2):
            flights[way][-1].wait_recv()
        yield [recv(way, count[way] - 1) for way in range(2)]

    owns = [own_a, own_b, own_c, own_d]

    def weight_piece(p, left, right):
        for i in range(TABLES // 2):
            value = dot(left[256 * i : 256 * i + 256, :], right, ((1,), (0,)))
            value = value.reshape(8, 32, RANK)
            if p == 0:
                for k in range(8):
                    own_a[k % NZL, 2 * i + k // NZL, 0:32, :] = value[k, :, 0:128]
                    own_a[k % NZL, 2 * i + k // NZL, 32:64, :] = value[k, :, 128:256]
                continue
            owns[p][8 * i : 8 * i + 8, 0:32, :] = value[:, :, 0:128]
            owns[p][8 * i : 8 * i + 8, 32:64, :] = value[:, :, 128:256]

    def piece_chain(p):
        return reduce_chain(
            p, NY, y,
            lambda dest: owns[p][pl.ds(dest * NZL, NZL)],
            lambda way, step: send_bcd.at[p - 1, way, step],
            lambda way, step: recv_bcd.at[p - 1, way, step],
            y_side,
        )

    def first_chain():
        near = zl + 1 - 2 * lax.rem(zl, 2)
        across = lax.rem(zl + 2, NZL)
        firsts = []
        for k, keeper in enumerate((lax.rem(near + 2, NZL), near)):
            near_send[k] = own_a[keeper].astype(BF16)
            firsts.append(links.copy(near_send.at[k], near_recv.at[k], rep_at(y, near)))
        yield
        firsts[0].wait_recv()
        across_send[...] = (own_a[across] + near_recv[0].astype(F32)).astype(BF16)
        second = links.copy(across_send, across_recv, rep_at(y, across))
        yield
        firsts[1].wait_recv()
        second.wait_recv()
        for k in range(NY):
            own_a[zl, k] += near_recv[1, k].astype(F32) + across_recv[k].astype(F32)
        yield from reduce_chain(
            0, NY, y,
            lambda dest: own_a[zl, dest],
            lambda way, step: send_a.at[way, step],
            lambda way, step: recv_a.at[way, step],
            y_side,
        )

    last = [None] * PIECES
    spreads = [[] for _ in range(PIECES)]

    def zl_stage(p, arrived):
        def value(where):
            return (
                owns[p][y * NZL + where]
                + arrived[0][where].astype(F32)
                + arrived[1][where].astype(F32)
            )

        for o in range(1, NZL):
            out, into = zl_send.at[p - 1, o - 1], zl_recv.at[p - 1, o - 1]
            out[...] = value(lax.rem(zl + o, NZL)).astype(BF16)
            spreads[p].append((links.copy(out, into, zl_peer[o - 1]), into))
        last[p] = value(zl)

    def finish(p):
        total = last[p]
        for copy, into in spreads[p]:
            copy.wait_recv()
            total = total + into[...].astype(F32)
        if p < 2:
            out = (expand_ref, reduce_ref)[p]
            out[:, 0:128] = total[0:32, :]
            out[:, 128:256] = total[32:64, :]
            if p == 0:
                line = total[64:65, :]
                picked = line[:, 0:32]
                for k in range(1, NZL):
                    picked = jnp.where(zl == k, line[:, 32 * k : 32 * k + 32], picked)
                gbias_ref[...] = picked
        else:
            for t in range(TPP):
                gtables_ref[(p - 2) * TPP + t] = total[16 * t : 16 * t + 16, :]

    handed[0].wait_recv()
    for t in range(TABLES):
        own_a[:, t, 64:80, :] = jnp.broadcast_to(
            biases[t : t + 1, :].reshape(1, 1, EMB), (NZL, 16, EMB)
        )
    weight_piece(0, gb_t, low[0])
    chains = [first_chain()] + [piece_chain(p) for p in range(1, PIECES)]
    next(chains[0])

    def cross(i, start):
        pair = slice(256 * i, 256 * i + 256)
        for c in range(HALF // 192):
            rows = pl.ds(pl.multiple_of(start + 192 * c, 64), 192)
            inner2 = dot(low[0, rows, :], ew_ref[pair, :], ((1,), (1,)))
            back2 = dot(low[1, rows, :], rw_ref[pair, :], ((1,), (1,)))
            for u in range(2):
                t = 2 * i + u
                columns = slice(t * EMB, (t + 1) * EMB)
                inner = inner2[:, u * EMB : (u + 1) * EMB] + bias_ref[t : t + 1, :]
                xf = pooled[rows, columns].astype(F32)
                crossed_ref[rows, columns] = (xf * inner + xf).astype(BF16)
                gf = cot_ref[rows, columns].astype(F32)
                grad = gf * (inner + 1.0) + back2[:, u * EMB : (u + 1) * EMB]
                spread[rows, columns] = (grad * inv_col[rows, t : t + 1]).astype(BF16)

    def table_piece(p):
        for k in range(TPP):
            t = (p - 2) * TPP + k
            value = dot(counts[t], spread[:, t * EMB : (t + 1) * EMB], ((1,), (0,)))
            owns[p][:, 16 * k : 16 * k + 16, :] = value.reshape(NREP, 16, EMB)

    cross(0, mine)
    cross(1, mine)
    handed[1].wait_recv()
    weight_piece(1, pooled_t, low[1])
    next(chains[1])
    cross(0, theirs)
    cross(1, theirs)
    table_piece(2)
    next(chains[2])
    next(chains[1])
    next(chains[0])
    cross(2, mine)
    cross(3, mine)
    next(chains[1])
    next(chains[2])
    cross(2, theirs)
    cross(3, theirs)
    table_piece(3)
    next(chains[3])
    next(chains[1])
    next(chains[2])
    next(chains[0])
    next(chains[3])
    zl_stage(1, next(chains[1]))
    next(chains[2])
    next(chains[0])
    next(chains[3])
    zl_stage(2, next(chains[2]))
    next(chains[0])
    next(chains[3])
    finish(1)
    next(chains[0])
    zl_stage(3, next(chains[3]))
    ends = next(chains[0])
    last[0] = own_a[zl, y] + ends[0][...].astype(F32) + ends[1][...].astype(F32)
    finish(0)
    finish(2)
    finish(3)
    for copy in links.sent:
        copy.wait_send()


def hand_out(*refs):
    sems = refs[10]
    copies = [pltpu.make_async_copy(refs[i], refs[5 + i], sems.at[i]) for i in range(5)]
    for copy in copies:
        copy.start()
    for copy in copies:
        copy.wait()


def body(tables, feature_ids, bag_lengths, reduce_weight, expand_weight, cross_bias, cotangent):
    vmem = pl.BlockSpec(memory_space=pltpu.VMEM)
    anywhere = pl.BlockSpec(memory_space=pl.ANY)
    kept = (
        ((GROUP, FEATURES), BF16),
        ((FEATURES // NREP, RANK), F32),
        ((FEATURES // NREP, RANK), F32),
        ((1, FEATURES // NREP), F32),
        ((TABLES, ROWS // NREP, EMB), F32),
    )
    made = pl.pallas_call(
        kernel,
        out_shape=tuple(pltpu.VMEM(*k) for k in kept),
        in_specs=[pl.BlockSpec(memory_space=pltpu.HBM)] * 7,
        out_specs=(vmem,) * 5,
        scratch_shapes=[
            pltpu.VMEM((TABLES, HOT, GROUP), jnp.int32),
            pltpu.VMEM((TABLES, GROUP), jnp.int32),
            pltpu.VMEM((TABLES, ROWS, EMB), BF16),
            pltpu.VMEM((GROUP, FEATURES), BF16),
            pltpu.VMEM((FEATURES, RANK), BF16),
            pltpu.VMEM((FEATURES, RANK), BF16),
            pltpu.VMEM((TABLES, EMB), F32),
            pltpu.SemaphoreType.DMA((7,)),
            pltpu.VMEM((TABLES, ROWS, GROUP), BF16),
            pltpu.VMEM((TABLES, EMB, ROWS), BF16),
            pltpu.VMEM((GROUP, FEATURES), BF16),
            pltpu.VMEM((FEATURES, GROUP), BF16),
            pltpu.VMEM((GROUP, FEATURES), BF16),
            pltpu.VMEM((FEATURES, GROUP), BF16),
            pltpu.VMEM((GROUP, FEATURES), BF16),
            pltpu.VMEM((GROUP, TABLES), F32),
            pltpu.VMEM((TABLES, GROUP), F32),
            pltpu.VMEM((TABLES, EMB), F32),
            pltpu.VMEM((2, HALF, RANK), BF16),
            pltpu.VMEM((2, HALF, RANK), BF16),
            pltpu.VMEM((2, NX, CHUNK, RANK), F32),
            pltpu.VMEM((2, 2, NX // 2, CHUNK, RANK), BF16),
            pltpu.VMEM((2, 2, NX // 2, CHUNK, RANK), BF16),
            pltpu.VMEM((2, CHUNK, RANK), BF16),
            pltpu.VMEM((2, CHUNK, RANK), BF16),
            pltpu.VMEM((2, GROUP, RANK), BF16),
            pltpu.VMEM((NZL, NY, TALL, EMB), F32),
            pltpu.VMEM((NREP, WIDE, EMB), F32),
            pltpu.VMEM((NREP, WIDE, EMB), F32),
            pltpu.VMEM((NREP, WIDE, EMB), F32),
            pltpu.VMEM((2, NY, TALL, EMB), BF16),
            pltpu.VMEM((2, NY, TALL, EMB), BF16),
            pltpu.VMEM((NY, TALL, EMB), BF16),
            pltpu.VMEM((NY, TALL, EMB), BF16),
            pltpu.VMEM((2, NY // 2, TALL, EMB), BF16),
            pltpu.VMEM((PIECES - 1, 2, NY // 2, NZL, WIDE, EMB), BF16),
            pltpu.VMEM((2, NY // 2, TALL, EMB), BF16),
            pltpu.VMEM((PIECES - 1, 2, NY // 2, NZL, WIDE, EMB), BF16),
            pltpu.VMEM((PIECES - 1, NZL - 1, WIDE, EMB), BF16),
            pltpu.VMEM((PIECES - 1, NZL - 1, WIDE, EMB), BF16),
            pltpu.SemaphoreType.DMA((COPIES,)),
            pltpu.SemaphoreType.DMA((COPIES,)),
        ],
        compiler_params=pltpu.CompilerParams(
            collective_id=0, has_side_effects=True, vmem_limit_bytes=62 << 20
        ),
        cost_estimate=pl.CostEstimate(
            flops=5 << 30, bytes_accessed=8 << 20, transcendentals=0
        ),
    )(
        jnp.transpose(feature_ids, (1, 2, 0)),
        bag_lengths.T,
        tables,
        cotangent,
        reduce_weight,
        expand_weight,
        cross_bias.reshape(TABLES, EMB),
    )
    crossed, grad_reduce, grad_expand, grad_bias, grad_tables = made
    return crossed, grad_reduce, grad_expand, grad_bias.reshape(-1), grad_tables


def solution(mesh):
    in_specs = (
        P("mp", None, None),
        P("replica", "mp", None),
        P("replica", "mp"),
        P("mp", None),
        P("mp", None),
        P("mp"),
        P("replica", "mp"),
    )
    out_specs = (
        P("replica", "mp"),
        P(("mp", "replica"), None),
        P(("mp", "replica"), None),
        P(("mp", "replica")),
        P("mp", "replica", None),
    )
    return jax.shard_map(body, mesh=mesh, in_specs=in_specs, out_specs=out_specs, check_vma=False)
```

```python
import jax
import jax.numpy as jnp
from jax import lax
from jax.experimental import pallas as pl
from jax.experimental.pallas import tpu as pltpu
from jax.sharding import PartitionSpec as P

NX, NZH, NCORE = 8, 2, 2
NY, NZL = 8, 4
NREP = NY * NZL
TABLES, ROWS, EMB, HOT = 8, 512, 128, 4
FEATURES, RANK = TABLES * EMB, 256
GROUP = 768
HALF = GROUP // NCORE
CHUNK = HALF // NX
PIECES = 4
TPP = 4
WIDE = 64
TALL = 80
FAR_FIRST = (4, 3, 5, 2, 6, 1, 7)
MESH = pl.DeviceIdType.MESH
BF16 = jnp.bfloat16
F32 = jnp.float32


def hops(part, way, n):
    far = n // 2
    return far if part % 2 == way else n - 1 - far


def dot(a, b, dims):
    return lax.dot_general(a, b, (dims, ((), ())), preferred_element_type=F32)


class Links:
    def __init__(self, send_sems, recv_sems):
        self.send_sems, self.recv_sems = send_sems, recv_sems
        self.used = 0
        self.sent = []

    def copy(self, src, dst, device):
        i = self.used
        self.used += 1
        made = pltpu.make_async_remote_copy(
            src_ref=src,
            dst_ref=dst,
            send_sem=self.send_sems.at[i],
            recv_sem=self.recv_sems.at[i],
            device_id=device,
            device_id_type=MESH,
        )
        made.start()
        self.sent.append(made)
        return made


COPIES = 2 + 14 + 2 + 14 + 2 + 3 + 7 * PIECES + 3 * (PIECES - 1)


def kernel(
    ids_hbm, lens_hbm, tables_hbm, cot_hbm, rw_hbm, ew_hbm, bias_hbm,
    crossed_ref, reduce_ref, expand_ref, gbias_ref, gtables_ref,
    ids_ref, lens_ref, tables_ref, cot_ref, rw_ref, ew_ref, bias_ref, load_sems,
    counts, tabs_t, pooled, pooled_t, gb, gb_t, spread, inv_col, inv_row, biases,
    core_send, core_recv, rank_own, rank_send, rank_recv, zh_send, zh_recv, low,
    own_a, own_b, own_c, own_d, near_send, near_recv, across_send, across_recv,
    send_a, send_bcd, recv_a, recv_bcd, zl_send, zl_recv,
    send_sems, recv_sems,
):
    m, r = lax.axis_index("mp"), lax.axis_index("replica")
    core, zh, x = lax.rem(m, 2), lax.rem(m // 2, 2), m // 4
    y, zl = r // NZL, lax.rem(r, NZL)

    def mp_at(xx, zz, cc):
        return {"mp": (xx * NZH + zz) * NCORE + cc}

    def rep_at(yy, zz):
        return {"replica": yy * NZL + zz}

    y_side = (rep_at(lax.rem(y + 1, NY), zl), rep_at(lax.rem(y + NY - 1, NY), zl))
    other_core, other_zh = mp_at(x, zh, 1 - core), mp_at(x, 1 - zh, core)
    y_peer = [rep_at(lax.rem(y + o, NY), zl) for o in range(1, NY)]
    zl_peer = [rep_at(y, lax.rem(zl + o, NZL)) for o in range(1, NZL)]

    x_at = [
        [x] + [lax.rem(x + o, NX) for o in range(1, 5)],
        [x] + [lax.rem(x + NX - o, NX) for o in range(1, 5)],
    ]
    x_dev = [[None] + [mp_at(x_at[way][o], zh, core) for o in (1, 2)] for way in range(2)]

    barrier = pltpu.get_barrier_semaphore()
    greeted = [*x_dev[0][1:], *x_dev[1][1:], *y_peer, other_core, other_zh, *zl_peer]
    for device in greeted:
        pl.semaphore_signal(barrier, inc=1, device_id=device, device_id_type=MESH)

    inputs = (ids_hbm, lens_hbm, tables_hbm, cot_hbm, rw_hbm, ew_hbm, bias_hbm)
    places = (ids_ref, lens_ref, tables_ref, cot_ref, rw_ref, ew_ref, bias_ref)
    loads = []
    for i in range(len(inputs)):
        loads.append(pltpu.make_async_copy(inputs[i], places[i], load_sems.at[i]))
        loads[i].start()

    links = Links(send_sems, recv_sems)

    loads[0].wait()
    loads[1].wait()
    inv_row[...] = 1.0 / lens_ref[...].astype(F32)
    inv_col[...] = jnp.transpose(inv_row[...])
    biases[...] = jnp.zeros_like(biases)

    def half(start, first):
        span = pl.ds(pl.multiple_of(start, 128), HALF)
        row_of = lax.broadcasted_iota(jnp.int32, (64, HALF), 0).astype(F32).astype(BF16)
        one, zero = jnp.ones((), BF16), jnp.zeros((64, HALF), BF16)
        for t in range(TABLES):
            lens = lens_ref[t : t + 1, span]
            picks = []
            for j in range(HOT):
                picks.append(jnp.where(lens > j, ids_ref[t, j : j + 1, span], -1))
            for c in range(ROWS // 64):
                total = zero
                for j in range(HOT):
                    pick = (picks[j] - 64 * c).astype(F32).astype(BF16)
                    total = jnp.where(row_of == pick, total + one, total)
                counts[t, 64 * c : 64 * c + 64, span] = total
            if first:
                if t == 0:
                    loads[2].wait()
                    loads[3].wait()
                tabs_t[t] = jnp.transpose(tables_ref[t])
            columns = slice(t * EMB, (t + 1) * EMB)
            sums = dot(tabs_t[t], counts[t, :, span], ((1,), (0,)))
            mean_t = (sums * inv_row[t : t + 1, span]).astype(BF16)
            pooled_t[columns, span] = mean_t
            mean = jnp.transpose(mean_t)
            pooled[pl.ds(start, HALF), columns] = mean
            grad = cot_ref[pl.ds(start, HALF), columns].astype(F32) * mean.astype(F32)
            gb[pl.ds(start, HALF), columns] = grad.astype(BF16)
            biases[t : t + 1, :] += jnp.sum(grad, axis=0, keepdims=True)
        if first:
            for i in range(4, 7):
                loads[i].wait()
        rows = pl.ds(start, HALF)
        return (
            dot(pooled[rows, :], rw_ref[...], ((1,), (0,))),
            dot(gb[rows, :], ew_ref[...], ((1,), (0,))),
        )

    theirs = pl.multiple_of((1 - core) * HALF, HALF)
    mine = pl.multiple_of(core * HALF, HALF)
    parts = half(theirs, True)
    for p in range(2):
        core_send[p] = parts[p].astype(BF16)
    pl.semaphore_wait(barrier, len(greeted))
    from_core = [
        links.copy(core_send.at[p], core_recv.at[p], other_core) for p in range(2)
    ]
    parts = half(mine, False)

    scatters = [{}, {}]
    gathers = [{}, {}]
    swaps = [None, None]
    summed = [None, None]
    handed = [None, None]

    def scatter(p, way, d, value, to):
        rank_send[p, way, d - 1] = value.astype(BF16)
        scatters[p][way, d] = links.copy(
            rank_send.at[p, way, d - 1], rank_recv.at[p, way, d - 1], x_dev[way][to]
        )

    def arrived(p, way, d):
        scatters[p][way, d].wait_recv()
        return rank_recv[p, way, d - 1].astype(F32)

    def scatter_first(p):
        from_core[p].wait_recv()
        rank_own[p] = (parts[p] + core_recv[p].astype(F32)).reshape(NX, CHUNK, RANK)
        for way in range(2):
            if hops(p, way, NX) == 4:
                scatter(p, way, 4, rank_own[p, x_at[way][4]], 2)
        for way in range(2):
            scatter(p, way, 3, rank_own[p, x_at[way][3]], 1)
        for way in range(2):
            scatter(p, way, 1, rank_own[p, x_at[way][1]], 1)

    def scatter_second(p):
        for way in range(2):
            value = rank_own[p, x_at[way][2]] + arrived(p, way, 3)
            if hops(p, way, NX) == 4:
                value = value + arrived(p, way, 4)
            scatter(p, way, 2, value, 2)

    def scatter_last(p):
        value = rank_own[p, x]
        for d in (1, 2):
            for way in range(2):
                value = value + arrived(p, way, d)
        summed[p] = value
        zh_send[p] = value.astype(BF16)
        swaps[p] = links.copy(zh_send.at[p], zh_recv.at[p], other_zh)

    def block(p, xx):
        return low.at[p, pl.ds(pl.multiple_of(mine + xx * CHUNK, 16), CHUNK), :]

    def gather_first(p):
        swaps[p].wait_recv()
        block(p, x)[...] = (summed[p] + zh_recv[p].astype(F32)).astype(BF16)
        for d in (2, 1):
            for way in range(2):
                gathers[p][way, d] = links.copy(block(p, x), block(p, x), x_dev[way][d])

    def gather_second(p):
        for way in range(2):
            source = block(p, x_at[1 - way][2])
            gathers[p][way, 2].wait_recv()
            for d in range(3, hops(p, way, NX) + 1):
                gathers[p][way, d] = links.copy(source, source, x_dev[way][d - 2])

    def gather_last(p):
        for (way, d), copy in gathers[p].items():
            if d != 2:
                copy.wait_recv()
        rows = low.at[p, pl.ds(mine, HALF), :]
        handed[p] = links.copy(rows, rows, other_core)

    def flip(t):
        gb_t[t * EMB : (t + 1) * EMB, :] = jnp.transpose(gb[:, t * EMB : (t + 1) * EMB])

    scatter_first(0)
    scatter_first(1)
    for t in range(TABLES // 2):
        flip(t)
    scatter_second(0)
    scatter_second(1)
    for t in range(TABLES // 2, TABLES):
        flip(t)
    scatter_last(0)
    scatter_last(1)
    gather_first(0)
    gather_first(1)
    gather_second(0)
    gather_second(1)
    gather_last(0)

    def reduce_chain(part, n, me, own, send, recv, sides):
        count = [hops(part, way, n) for way in range(2)]
        flights = [[], []]
        for step in range(max(count)):
            for way in range(2):
                if step >= count[way]:
                    continue
                d = count[way] - step
                dest = lax.rem(me + d, n) if way == 0 else lax.rem(me + n - d, n)
                value = own(dest)
                if step > 0:
                    flights[way][step - 1].wait_recv()
                    value = value + recv(way, step - 1)[...].astype(F32)
                send(way, step)[...] = value.astype(BF16)
                flights[way].append(links.copy(send(way, step), recv(way, step), sides[way]))
            yield
        for way in range(2):
            flights[way][-1].wait_recv()
        yield [recv(way, count[way] - 1) for way in range(2)]

    owns = [own_a, own_b, own_c, own_d]

    def weight_piece(p, left, right):
        for i in range(TABLES // 2):
            value = dot(left[256 * i : 256 * i + 256, :], right, ((1,), (0,)))
            value = value.reshape(8, 32, RANK)
            if p == 0:
                for k in range(8):
                    own_a[k % NZL, 2 * i + k // NZL, 0:32, :] = value[k, :, 0:128]
                    own_a[k % NZL, 2 * i + k // NZL, 32:64, :] = value[k, :, 128:256]
                continue
            owns[p][8 * i : 8 * i + 8, 0:32, :] = value[:, :, 0:128]
            owns[p][8 * i : 8 * i + 8, 32:64, :] = value[:, :, 128:256]

    def piece_chain(p):
        return reduce_chain(
            p, NY, y,
            lambda dest: owns[p][pl.ds(dest * NZL, NZL)],
            lambda way, step: send_bcd.at[p - 1, way, step],
            lambda way, step: recv_bcd.at[p - 1, way, step],
            y_side,
        )

    def first_chain():
        near = zl + 1 - 2 * lax.rem(zl, 2)
        across = lax.rem(zl + 2, NZL)
        firsts = []
        for k, keeper in enumerate((lax.rem(near + 2, NZL), near)):
            near_send[k] = own_a[keeper].astype(BF16)
            firsts.append(links.copy(near_send.at[k], near_recv.at[k], rep_at(y, near)))
        yield
        firsts[0].wait_recv()
        across_send[...] = (own_a[across] + near_recv[0].astype(F32)).astype(BF16)
        second = links.copy(across_send, across_recv, rep_at(y, across))
        yield
        firsts[1].wait_recv()
        second.wait_recv()
        for k in range(NY):
            own_a[zl, k] += near_recv[1, k].astype(F32) + across_recv[k].astype(F32)
        rounds = []
        for o in FAR_FIRST:
            send_a[o - 1] = own_a[zl, lax.rem(y + o, NY)].astype(BF16)
            rounds.append(links.copy(send_a.at[o - 1], recv_a.at[o - 1], y_peer[o - 1]))
        yield
        total = own_a[zl, y]
        for copy, o in zip(rounds, FAR_FIRST, strict=True):
            copy.wait_recv()
            total = total + recv_a[o - 1].astype(F32)
        yield total

    last = [None] * PIECES
    spreads = [[] for _ in range(PIECES)]

    def zl_stage(p, arrived):
        def value(where):
            return (
                owns[p][y * NZL + where]
                + arrived[0][where].astype(F32)
                + arrived[1][where].astype(F32)
            )

        for o in range(1, NZL):
            out, into = zl_send.at[p - 1, o - 1], zl_recv.at[p - 1, o - 1]
            out[...] = value(lax.rem(zl + o, NZL)).astype(BF16)
            spreads[p].append((links.copy(out, into, zl_peer[o - 1]), into))
        last[p] = value(zl)

    def finish(p):
        total = last[p]
        for copy, into in spreads[p]:
            copy.wait_recv()
            total = total + into[...].astype(F32)
        if p < 2:
            out = (expand_ref, reduce_ref)[p]
            out[:, 0:128] = total[0:32, :]
            out[:, 128:256] = total[32:64, :]
            if p == 0:
                line = total[64:65, :]
                picked = line[:, 0:32]
                for k in range(1, NZL):
                    picked = jnp.where(zl == k, line[:, 32 * k : 32 * k + 32], picked)
                gbias_ref[...] = picked
        else:
            for t in range(TPP):
                gtables_ref[(p - 2) * TPP + t] = total[16 * t : 16 * t + 16, :]

    handed[0].wait_recv()
    for t in range(TABLES):
        own_a[:, t, 64:80, :] = jnp.broadcast_to(
            biases[t : t + 1, :].reshape(1, 1, EMB), (NZL, 16, EMB)
        )
    weight_piece(0, gb_t, low[0])
    chains = [first_chain()] + [piece_chain(p) for p in range(1, PIECES)]
    next(chains[0])

    def cross(i, start):
        pair = slice(256 * i, 256 * i + 256)
        for c in range(HALF // 192):
            rows = pl.ds(pl.multiple_of(start + 192 * c, 64), 192)
            inner2 = dot(low[0, rows, :], ew_ref[pair, :], ((1,), (1,)))
            back2 = dot(low[1, rows, :], rw_ref[pair, :], ((1,), (1,)))
            for u in range(2):
                t = 2 * i + u
                columns = slice(t * EMB, (t + 1) * EMB)
                inner = inner2[:, u * EMB : (u + 1) * EMB] + bias_ref[t : t + 1, :]
                xf = pooled[rows, columns].astype(F32)
                crossed_ref[rows, columns] = (xf * inner + xf).astype(BF16)
                gf = cot_ref[rows, columns].astype(F32)
                grad = gf * (inner + 1.0) + back2[:, u * EMB : (u + 1) * EMB]
                spread[rows, columns] = (grad * inv_col[rows, t : t + 1]).astype(BF16)

    def table_piece(p):
        for k in range(TPP):
            t = (p - 2) * TPP + k
            value = dot(counts[t], spread[:, t * EMB : (t + 1) * EMB], ((1,), (0,)))
            owns[p][:, 16 * k : 16 * k + 16, :] = value.reshape(NREP, 16, EMB)

    gather_last(1)
    cross(0, mine)
    cross(1, mine)
    handed[1].wait_recv()
    weight_piece(1, pooled_t, low[1])
    next(chains[1])
    cross(0, theirs)
    cross(1, theirs)
    table_piece(2)
    next(chains[2])
    next(chains[1])
    for start in (mine, theirs):
        cross(2, start)
        cross(3, start)
    table_piece(3)
    next(chains[3])
    next(chains[2])
    next(chains[1])
    next(chains[0])
    next(chains[3])
    next(chains[2])
    next(chains[1])
    next(chains[3])
    next(chains[2])
    next(chains[0])
    zl_stage(1, next(chains[1]))
    next(chains[3])
    zl_stage(2, next(chains[2]))
    finish(1)
    last[0] = next(chains[0])
    zl_stage(3, next(chains[3]))
    finish(0)
    finish(2)
    finish(3)
    for copy in links.sent:
        copy.wait_send()


def hand_out(*refs):
    for i in range(4):
        refs[4 + i][...] = refs[i][...]


def body(tables, feature_ids, bag_lengths, reduce_weight, expand_weight, cross_bias, cotangent):
    vmem = pl.BlockSpec(memory_space=pltpu.VMEM)
    anywhere = pl.BlockSpec(memory_space=pl.ANY)
    kept = (
        ((GROUP, FEATURES), BF16),
        ((FEATURES // NREP, RANK), F32),
        ((FEATURES // NREP, RANK), F32),
        ((1, FEATURES // NREP), F32),
        ((TABLES, ROWS // NREP, EMB), F32),
    )
    made = pl.pallas_call(
        kernel,
        out_shape=tuple(pltpu.VMEM(*k) for k in kept),
        in_specs=[pl.BlockSpec(memory_space=pltpu.HBM)] * 7,
        out_specs=(vmem,) * 5,
        scratch_shapes=[
            pltpu.VMEM((TABLES, HOT, GROUP), jnp.int32),
            pltpu.VMEM((TABLES, GROUP), jnp.int32),
            pltpu.VMEM((TABLES, ROWS, EMB), BF16),
            pltpu.VMEM((GROUP, FEATURES), BF16),
            pltpu.VMEM((FEATURES, RANK), BF16),
            pltpu.VMEM((FEATURES, RANK), BF16),
            pltpu.VMEM((TABLES, EMB), F32),
            pltpu.SemaphoreType.DMA((7,)),
            pltpu.VMEM((TABLES, ROWS, GROUP), BF16),
            pltpu.VMEM((TABLES, EMB, ROWS), BF16),
            pltpu.VMEM((GROUP, FEATURES), BF16),
            pltpu.VMEM((FEATURES, GROUP), BF16),
            pltpu.VMEM((GROUP, FEATURES), BF16),
            pltpu.VMEM((FEATURES, GROUP), BF16),
            pltpu.VMEM((GROUP, FEATURES), BF16),
            pltpu.VMEM((GROUP, TABLES), F32),
            pltpu.VMEM((TABLES, GROUP), F32),
            pltpu.VMEM((TABLES, EMB), F32),
            pltpu.VMEM((2, HALF, RANK), BF16),
            pltpu.VMEM((2, HALF, RANK), BF16),
            pltpu.VMEM((2, NX, CHUNK, RANK), F32),
            pltpu.VMEM((2, 2, NX // 2, CHUNK, RANK), BF16),
            pltpu.VMEM((2, 2, NX // 2, CHUNK, RANK), BF16),
            pltpu.VMEM((2, CHUNK, RANK), BF16),
            pltpu.VMEM((2, CHUNK, RANK), BF16),
            pltpu.VMEM((2, GROUP, RANK), BF16),
            pltpu.VMEM((NZL, NY, TALL, EMB), F32),
            pltpu.VMEM((NREP, WIDE, EMB), F32),
            pltpu.VMEM((NREP, WIDE, EMB), F32),
            pltpu.VMEM((NREP, WIDE, EMB), F32),
            pltpu.VMEM((2, NY, TALL, EMB), BF16),
            pltpu.VMEM((2, NY, TALL, EMB), BF16),
            pltpu.VMEM((NY, TALL, EMB), BF16),
            pltpu.VMEM((NY, TALL, EMB), BF16),
            pltpu.VMEM((NY - 1, TALL, EMB), BF16),
            pltpu.VMEM((PIECES - 1, 2, NY // 2, NZL, WIDE, EMB), BF16),
            pltpu.VMEM((NY - 1, TALL, EMB), BF16),
            pltpu.VMEM((PIECES - 1, 2, NY // 2, NZL, WIDE, EMB), BF16),
            pltpu.VMEM((PIECES - 1, NZL - 1, WIDE, EMB), BF16),
            pltpu.VMEM((PIECES - 1, NZL - 1, WIDE, EMB), BF16),
            pltpu.SemaphoreType.DMA((COPIES,)),
            pltpu.SemaphoreType.DMA((COPIES,)),
        ],
        compiler_params=pltpu.CompilerParams(
            collective_id=0, has_side_effects=True, vmem_limit_bytes=62 << 20
        ),
        cost_estimate=pl.CostEstimate(
            flops=5 << 30, bytes_accessed=8 << 20, transcendentals=0
        ),
    )(
        jnp.transpose(feature_ids, (1, 2, 0)),
        bag_lengths.T,
        tables,
        cotangent,
        reduce_weight,
        expand_weight,
        cross_bias.reshape(TABLES, EMB),
    )
    crossed = made[0]
    grad_reduce, grad_expand, grad_bias, grad_tables = pl.pallas_call(
        hand_out,
        out_shape=tuple(jax.ShapeDtypeStruct(*k) for k in kept[1:]),
        in_specs=[vmem] * 4,
        out_specs=(vmem,) * 4,
    )(*made[1:])
    return crossed, grad_reduce, grad_expand, grad_bias.reshape(-1), grad_tables


def solution(mesh):
    in_specs = (
        P("mp", None, None),
        P("replica", "mp", None),
        P("replica", "mp"),
        P("mp", None),
        P("mp", None),
        P("mp"),
        P("replica", "mp"),
    )
    out_specs = (
        P("replica", "mp"),
        P(("mp", "replica"), None),
        P(("mp", "replica"), None),
        P(("mp", "replica")),
        P("mp", "replica", None),
    )
    return jax.shard_map(body, mesh=mesh, in_specs=in_specs, out_specs=out_specs, check_vma=False)
```

```python
import jax
import jax.numpy as jnp
from jax import lax
from jax.experimental import pallas as pl
from jax.experimental.pallas import tpu as pltpu
from jax.sharding import PartitionSpec as P

NX, NZH, NCORE = 8, 2, 2
NY, NZL = 8, 4
NREP = NY * NZL
TABLES, ROWS, EMB, HOT = 8, 512, 128, 4
FEATURES, RANK = TABLES * EMB, 256
GROUP = 768
HALF = GROUP // NCORE
CHUNK = HALF // NX
PIECES = 4
TPP = 4
WIDE = 64
TALL = 80
LINES = NY * WIDE
FAR_FIRST = (4, 3, 5, 2, 6, 1, 7)
MESH = pl.DeviceIdType.MESH
BF16 = jnp.bfloat16
F32 = jnp.float32


def hops(part, way, n):
    far = n // 2
    return far if part % 2 == way else n - 1 - far


def dot(a, b, dims):
    return lax.dot_general(a, b, (dims, ((), ())), preferred_element_type=F32)


class Links:
    def __init__(self, send_sems, recv_sems):
        self.send_sems, self.recv_sems = send_sems, recv_sems
        self.used = 0
        self.sent = []

    def copy(self, src, dst, device):
        i = self.used
        self.used += 1
        made = pltpu.make_async_remote_copy(
            src_ref=src,
            dst_ref=dst,
            send_sem=self.send_sems.at[i],
            recv_sem=self.recv_sems.at[i],
            device_id=device,
            device_id_type=MESH,
        )
        made.start()
        self.sent.append(made)
        return made


COPIES = 2 + 14 + 2 + 14 + 2 + 3 + 7 * PIECES + 3 * (PIECES - 1)


def kernel(
    ids_hbm, lens_hbm, tables_hbm, cot_hbm, rw_hbm, ew_hbm, bias_hbm,
    crossed_ref, reduce_ref, expand_ref, gbias_ref, gtables_ref,
    ids_ref, lens_ref, tables_ref, cot_ref, rw_ref, ew_ref, bias_ref, load_sems,
    counts, tabs_t, pooled, pooled_t, gb, gb_t, spread, inv_col, inv_row, biases,
    core_send, core_recv, rank_own, rank_send, rank_recv, zh_send, zh_recv, low,
    own_a, own_b, own_c, own_d, near_send, near_recv, across_send, across_recv,
    send_a, send_bcd, recv_a, recv_bcd, zl_send, zl_recv,
    send_sems, recv_sems,
):
    m, r = lax.axis_index("mp"), lax.axis_index("replica")
    core, zh, x = lax.rem(m, 2), lax.rem(m // 2, 2), m // 4
    y, zl = r // NZL, lax.rem(r, NZL)

    def mp_at(xx, zz, cc):
        return {"mp": (xx * NZH + zz) * NCORE + cc}

    def rep_at(yy, zz):
        return {"replica": yy * NZL + zz}

    y_side = (rep_at(lax.rem(y + 1, NY), zl), rep_at(lax.rem(y + NY - 1, NY), zl))
    other_core, other_zh = mp_at(x, zh, 1 - core), mp_at(x, 1 - zh, core)
    y_peer = [rep_at(lax.rem(y + o, NY), zl) for o in range(1, NY)]
    zl_peer = [rep_at(y, lax.rem(zl + o, NZL)) for o in range(1, NZL)]

    x_at = [
        [x] + [lax.rem(x + o, NX) for o in range(1, 5)],
        [x] + [lax.rem(x + NX - o, NX) for o in range(1, 5)],
    ]
    x_dev = [[None] + [mp_at(x_at[way][o], zh, core) for o in (1, 2)] for way in range(2)]

    barrier = pltpu.get_barrier_semaphore()
    greeted = [*x_dev[0][1:], *x_dev[1][1:], *y_peer, other_core, other_zh, *zl_peer]
    for device in greeted:
        pl.semaphore_signal(barrier, inc=1, device_id=device, device_id_type=MESH)

    inputs = (ids_hbm, lens_hbm, tables_hbm, cot_hbm, rw_hbm, ew_hbm, bias_hbm)
    places = (ids_ref, lens_ref, tables_ref, cot_ref, rw_ref, ew_ref, bias_ref)
    loads = []
    for i in range(len(inputs)):
        loads.append(pltpu.make_async_copy(inputs[i], places[i], load_sems.at[i]))
        loads[i].start()

    links = Links(send_sems, recv_sems)

    loads[0].wait()
    loads[1].wait()
    inv_row[...] = 1.0 / lens_ref[...].astype(F32)
    inv_col[...] = jnp.transpose(inv_row[...])
    biases[...] = jnp.zeros_like(biases)

    def half(start, first):
        span = pl.ds(pl.multiple_of(start, 128), HALF)
        row_of = lax.broadcasted_iota(jnp.int32, (64, HALF), 0).astype(F32).astype(BF16)
        one, zero = jnp.ones((), BF16), jnp.zeros((64, HALF), BF16)
        for t in range(TABLES):
            lens = lens_ref[t : t + 1, span]
            picks = []
            for j in range(HOT):
                picks.append(jnp.where(lens > j, ids_ref[t, j : j + 1, span], -1))
            for c in range(ROWS // 64):
                total = zero
                for j in range(HOT):
                    pick = (picks[j] - 64 * c).astype(F32).astype(BF16)
                    total = jnp.where(row_of == pick, total + one, total)
                counts[t, 64 * c : 64 * c + 64, span] = total
            if first:
                if t == 0:
                    loads[2].wait()
                    loads[3].wait()
                tabs_t[t] = jnp.transpose(tables_ref[t])
            columns = slice(t * EMB, (t + 1) * EMB)
            sums = dot(tabs_t[t], counts[t, :, span], ((1,), (0,)))
            mean_t = (sums * inv_row[t : t + 1, span]).astype(BF16)
            pooled_t[columns, span] = mean_t
            mean = jnp.transpose(mean_t)
            pooled[pl.ds(start, HALF), columns] = mean
            grad = cot_ref[pl.ds(start, HALF), columns].astype(F32) * mean.astype(F32)
            gb[pl.ds(start, HALF), columns] = grad.astype(BF16)
            biases[t : t + 1, :] += jnp.sum(grad, axis=0, keepdims=True)
        if first:
            for i in range(4, 7):
                loads[i].wait()
        rows = pl.ds(start, HALF)
        return (
            dot(pooled[rows, :], rw_ref[...], ((1,), (0,))),
            dot(gb[rows, :], ew_ref[...], ((1,), (0,))),
        )

    theirs = pl.multiple_of((1 - core) * HALF, HALF)
    mine = pl.multiple_of(core * HALF, HALF)
    parts = half(theirs, True)
    for p in range(2):
        core_send[p] = parts[p].astype(BF16)
    pl.semaphore_wait(barrier, len(greeted))
    from_core = [
        links.copy(core_send.at[p], core_recv.at[p], other_core) for p in range(2)
    ]
    parts = half(mine, False)

    scatters = [{}, {}]
    gathers = [{}, {}]
    swaps = [None, None]
    summed = [None, None]
    handed = [None, None]

    def scatter(p, way, d, value, to):
        rank_send[p, way, d - 1] = value.astype(BF16)
        scatters[p][way, d] = links.copy(
            rank_send.at[p, way, d - 1], rank_recv.at[p, way, d - 1], x_dev[way][to]
        )

    def arrived(p, way, d):
        scatters[p][way, d].wait_recv()
        return rank_recv[p, way, d - 1].astype(F32)

    def scatter_first(p):
        from_core[p].wait_recv()
        rank_own[p] = (parts[p] + core_recv[p].astype(F32)).reshape(NX, CHUNK, RANK)
        for way in range(2):
            if hops(p, way, NX) == 4:
                scatter(p, way, 4, rank_own[p, x_at[way][4]], 2)
        for way in range(2):
            scatter(p, way, 3, rank_own[p, x_at[way][3]], 1)
        for way in range(2):
            scatter(p, way, 1, rank_own[p, x_at[way][1]], 1)

    def scatter_second(p):
        for way in range(2):
            value = rank_own[p, x_at[way][2]] + arrived(p, way, 3)
            if hops(p, way, NX) == 4:
                value = value + arrived(p, way, 4)
            scatter(p, way, 2, value, 2)

    def scatter_last(p):
        value = rank_own[p, x]
        for d in (1, 2):
            for way in range(2):
                value = value + arrived(p, way, d)
        summed[p] = value
        zh_send[p] = value.astype(BF16)
        swaps[p] = links.copy(zh_send.at[p], zh_recv.at[p], other_zh)

    def block(p, xx):
        return low.at[p, pl.ds(pl.multiple_of(mine + xx * CHUNK, 16), CHUNK), :]

    def gather_first(p):
        swaps[p].wait_recv()
        block(p, x)[...] = (summed[p] + zh_recv[p].astype(F32)).astype(BF16)
        for d in (2, 1):
            for way in range(2):
                gathers[p][way, d] = links.copy(block(p, x), block(p, x), x_dev[way][d])

    def gather_second(p):
        for way in range(2):
            source = block(p, x_at[1 - way][2])
            gathers[p][way, 2].wait_recv()
            for d in range(3, hops(p, way, NX) + 1):
                gathers[p][way, d] = links.copy(source, source, x_dev[way][d - 2])

    def gather_last(p):
        for (way, d), copy in gathers[p].items():
            if d != 2:
                copy.wait_recv()
        rows = low.at[p, pl.ds(mine, HALF), :]
        handed[p] = links.copy(rows, rows, other_core)

    def flip(t):
        gb_t[t * EMB : (t + 1) * EMB, :] = jnp.transpose(gb[:, t * EMB : (t + 1) * EMB])

    scatter_first(0)
    scatter_first(1)
    for t in range(TABLES // 2):
        flip(t)
    scatter_second(0)
    scatter_second(1)
    for t in range(TABLES // 2, TABLES):
        flip(t)
    scatter_last(0)
    scatter_last(1)
    gather_first(0)
    gather_first(1)
    gather_second(0)
    gather_second(1)
    gather_last(0)

    def reduce_chain(part, n, me, own, send, recv, sides):
        count = [hops(part, way, n) for way in range(2)]
        flights = [[], []]
        for step in range(max(count)):
            for way in range(2):
                if step >= count[way]:
                    continue
                d = count[way] - step
                dest = lax.rem(me + d, n) if way == 0 else lax.rem(me + n - d, n)
                value = own(dest)
                if step > 0:
                    flights[way][step - 1].wait_recv()
                    value = value + recv(way, step - 1)[...].astype(F32)
                send(way, step)[...] = value.astype(BF16)
                flights[way].append(links.copy(send(way, step), recv(way, step), sides[way]))
            yield
        for way in range(2):
            flights[way][-1].wait_recv()
        yield [recv(way, count[way] - 1) for way in range(2)]

    owns = [own_a, own_b, own_c, own_d]

    def weight_piece(p, left, right):
        for i in range(TABLES // 2):
            value = dot(left[256 * i : 256 * i + 256, :], right, ((1,), (0,)))
            value = value.reshape(8, 32, RANK)
            if p == 0:
                for k in range(8):
                    own_a[k % NZL, 2 * i + k // NZL, 0:32, :] = value[k, :, 0:128]
                    own_a[k % NZL, 2 * i + k // NZL, 32:64, :] = value[k, :, 128:256]
                continue
            owns[p][8 * i : 8 * i + 8, 0:32, :] = value[:, :, 0:128]
            owns[p][8 * i : 8 * i + 8, 32:64, :] = value[:, :, 128:256]

    def piece_chain(p):
        return reduce_chain(
            p, NY, y,
            lambda dest: owns[p][pl.ds(dest * NZL, NZL)],
            lambda way, step: send_bcd.at[p - 1, way, step],
            lambda way, step: recv_bcd.at[p - 1, way, step],
            y_side,
        )

    def first_chain():
        near = zl + 1 - 2 * lax.rem(zl, 2)
        across = lax.rem(zl + 2, NZL)
        firsts = []
        for k, keeper in enumerate((lax.rem(near + 2, NZL), near)):
            near_send[k, 0:LINES] = own_a[keeper].reshape(LINES, EMB).astype(BF16)
            near_send[k, LINES:] = jnp.concatenate([biases[...]] * 2, axis=0).astype(BF16)
            firsts.append(links.copy(near_send.at[k], near_recv.at[k], rep_at(y, near)))
        yield
        firsts[0].wait_recv()
        across_send[0:LINES] = (
            own_a[across].reshape(LINES, EMB) + near_recv[0, 0:LINES].astype(F32)
        ).astype(BF16)
        biases[...] += near_recv[0, LINES:].astype(F32)[0:TABLES]
        across_send[LINES:] = jnp.concatenate([biases[...]] * 2, axis=0).astype(BF16)
        second = links.copy(across_send, across_recv, rep_at(y, across))
        yield
        firsts[1].wait_recv()
        second.wait_recv()
        for k in range(NY):
            rows = slice(k * WIDE, (k + 1) * WIDE)
            own_a[zl, k] += near_recv[1, rows].astype(F32) + across_recv[rows].astype(F32)
        biases[...] += across_recv[LINES:].astype(F32)[0:TABLES]

        def tall(where):
            line = jnp.broadcast_to(biases[pl.ds(where, 1), :], (TALL - WIDE, EMB))
            return jnp.concatenate([own_a[zl, where], line], axis=0)

        rounds = []
        for o in FAR_FIRST:
            send_a[o - 1] = tall(lax.rem(y + o, NY)).astype(BF16)
            rounds.append(links.copy(send_a.at[o - 1], recv_a.at[o - 1], y_peer[o - 1]))
        yield
        total = tall(y)
        for copy, o in zip(rounds, FAR_FIRST, strict=True):
            copy.wait_recv()
            total = total + recv_a[o - 1].astype(F32)
        yield total

    last = [None] * PIECES
    spreads = [[] for _ in range(PIECES)]

    def zl_stage(p, arrived):
        def value(where):
            return (
                owns[p][y * NZL + where]
                + arrived[0][where].astype(F32)
                + arrived[1][where].astype(F32)
            )

        for o in range(1, NZL):
            out, into = zl_send.at[p - 1, o - 1], zl_recv.at[p - 1, o - 1]
            out[...] = value(lax.rem(zl + o, NZL)).astype(BF16)
            spreads[p].append((links.copy(out, into, zl_peer[o - 1]), into))
        last[p] = value(zl)

    def finish(p):
        total = last[p]
        for copy, into in spreads[p]:
            copy.wait_recv()
            total = total + into[...].astype(F32)
        if p < 2:
            out = (expand_ref, reduce_ref)[p]
            out[:, 0:128] = total[0:32, :]
            out[:, 128:256] = total[32:64, :]
            if p == 0:
                line = total[64:65, :]
                picked = line[:, 0:32]
                for k in range(1, NZL):
                    picked = jnp.where(zl == k, line[:, 32 * k : 32 * k + 32], picked)
                gbias_ref[...] = picked
        else:
            for t in range(TPP):
                gtables_ref[(p - 2) * TPP + t] = total[16 * t : 16 * t + 16, :]

    handed[0].wait_recv()
    weight_piece(0, gb_t, low[0])
    chains = [first_chain()] + [piece_chain(p) for p in range(1, PIECES)]
    next(chains[0])

    def cross(i, start):
        pair = slice(256 * i, 256 * i + 256)
        for c in range(HALF // 192):
            rows = pl.ds(pl.multiple_of(start + 192 * c, 64), 192)
            inner2 = dot(low[0, rows, :], ew_ref[pair, :], ((1,), (1,)))
            back2 = dot(low[1, rows, :], rw_ref[pair, :], ((1,), (1,)))
            for u in range(2):
                t = 2 * i + u
                columns = slice(t * EMB, (t + 1) * EMB)
                inner = inner2[:, u * EMB : (u + 1) * EMB] + bias_ref[t : t + 1, :]
                xf = pooled[rows, columns].astype(F32)
                crossed_ref[rows, columns] = (xf * inner + xf).astype(BF16)
                gf = cot_ref[rows, columns].astype(F32)
                grad = gf * (inner + 1.0) + back2[:, u * EMB : (u + 1) * EMB]
                spread[rows, columns] = (grad * inv_col[rows, t : t + 1]).astype(BF16)

    def table_piece(p):
        for k in range(TPP):
            t = (p - 2) * TPP + k
            value = dot(counts[t], spread[:, t * EMB : (t + 1) * EMB], ((1,), (0,)))
            owns[p][:, 16 * k : 16 * k + 16, :] = value.reshape(NREP, 16, EMB)

    gather_last(1)
    cross(0, mine)
    cross(1, mine)
    handed[1].wait_recv()
    weight_piece(1, pooled_t, low[1])
    next(chains[1])
    cross(0, theirs)
    cross(1, theirs)
    table_piece(2)
    next(chains[2])
    next(chains[1])
    for start in (mine, theirs):
        cross(2, start)
        cross(3, start)
    table_piece(3)
    next(chains[3])
    next(chains[2])
    next(chains[1])
    next(chains[0])
    next(chains[3])
    next(chains[2])
    next(chains[1])
    next(chains[3])
    next(chains[2])
    next(chains[0])
    zl_stage(1, next(chains[1]))
    next(chains[3])
    zl_stage(2, next(chains[2]))
    finish(1)
    last[0] = next(chains[0])
    zl_stage(3, next(chains[3]))
    finish(0)
    finish(2)
    finish(3)
    for copy in links.sent:
        copy.wait_send()


def hand_out(*refs):
    for i in range(4):
        refs[4 + i][...] = refs[i][...]


def body(tables, feature_ids, bag_lengths, reduce_weight, expand_weight, cross_bias, cotangent):
    vmem = pl.BlockSpec(memory_space=pltpu.VMEM)
    anywhere = pl.BlockSpec(memory_space=pl.ANY)
    kept = (
        ((GROUP, FEATURES), BF16),
        ((FEATURES // NREP, RANK), F32),
        ((FEATURES // NREP, RANK), F32),
        ((1, FEATURES // NREP), F32),
        ((TABLES, ROWS // NREP, EMB), F32),
    )
    made = pl.pallas_call(
        kernel,
        out_shape=tuple(pltpu.VMEM(*k) for k in kept),
        in_specs=[pl.BlockSpec(memory_space=pltpu.HBM)] * 7,
        out_specs=(vmem,) * 5,
        scratch_shapes=[
            pltpu.VMEM((TABLES, HOT, GROUP), jnp.int32),
            pltpu.VMEM((TABLES, GROUP), jnp.int32),
            pltpu.VMEM((TABLES, ROWS, EMB), BF16),
            pltpu.VMEM((GROUP, FEATURES), BF16),
            pltpu.VMEM((FEATURES, RANK), BF16),
            pltpu.VMEM((FEATURES, RANK), BF16),
            pltpu.VMEM((TABLES, EMB), F32),
            pltpu.SemaphoreType.DMA((7,)),
            pltpu.VMEM((TABLES, ROWS, GROUP), BF16),
            pltpu.VMEM((TABLES, EMB, ROWS), BF16),
            pltpu.VMEM((GROUP, FEATURES), BF16),
            pltpu.VMEM((FEATURES, GROUP), BF16),
            pltpu.VMEM((GROUP, FEATURES), BF16),
            pltpu.VMEM((FEATURES, GROUP), BF16),
            pltpu.VMEM((GROUP, FEATURES), BF16),
            pltpu.VMEM((GROUP, TABLES), F32),
            pltpu.VMEM((TABLES, GROUP), F32),
            pltpu.VMEM((TABLES, EMB), F32),
            pltpu.VMEM((2, HALF, RANK), BF16),
            pltpu.VMEM((2, HALF, RANK), BF16),
            pltpu.VMEM((2, NX, CHUNK, RANK), F32),
            pltpu.VMEM((2, 2, NX // 2, CHUNK, RANK), BF16),
            pltpu.VMEM((2, 2, NX // 2, CHUNK, RANK), BF16),
            pltpu.VMEM((2, CHUNK, RANK), BF16),
            pltpu.VMEM((2, CHUNK, RANK), BF16),
            pltpu.VMEM((2, GROUP, RANK), BF16),
            pltpu.VMEM((NZL, NY, WIDE, EMB), F32),
            pltpu.VMEM((NREP, WIDE, EMB), F32),
            pltpu.VMEM((NREP, WIDE, EMB), F32),
            pltpu.VMEM((NREP, WIDE, EMB), F32),
            pltpu.VMEM((2, LINES + 16, EMB), BF16),
            pltpu.VMEM((2, LINES + 16, EMB), BF16),
            pltpu.VMEM((LINES + 16, EMB), BF16),
            pltpu.VMEM((LINES + 16, EMB), BF16),
            pltpu.VMEM((NY - 1, TALL, EMB), BF16),
            pltpu.VMEM((PIECES - 1, 2, NY // 2, NZL, WIDE, EMB), BF16),
            pltpu.VMEM((NY - 1, TALL, EMB), BF16),
            pltpu.VMEM((PIECES - 1, 2, NY // 2, NZL, WIDE, EMB), BF16),
            pltpu.VMEM((PIECES - 1, NZL - 1, WIDE, EMB), BF16),
            pltpu.VMEM((PIECES - 1, NZL - 1, WIDE, EMB), BF16),
            pltpu.SemaphoreType.DMA((COPIES,)),
            pltpu.SemaphoreType.DMA((COPIES,)),
        ],
        compiler_params=pltpu.CompilerParams(
            collective_id=0, has_side_effects=True, vmem_limit_bytes=62 << 20
        ),
        cost_estimate=pl.CostEstimate(
            flops=5 << 30, bytes_accessed=8 << 20, transcendentals=0
        ),
    )(
        jnp.transpose(feature_ids, (1, 2, 0)),
        bag_lengths.T,
        tables,
        cotangent,
        reduce_weight,
        expand_weight,
        cross_bias.reshape(TABLES, EMB),
    )
    crossed = made[0]
    grad_reduce, grad_expand, grad_bias, grad_tables = pl.pallas_call(
        hand_out,
        out_shape=tuple(jax.ShapeDtypeStruct(*k) for k in kept[1:]),
        in_specs=[vmem] * 4,
        out_specs=(vmem,) * 4,
    )(*made[1:])
    return crossed, grad_reduce, grad_expand, grad_bias.reshape(-1), grad_tables


def solution(mesh):
    in_specs = (
        P("mp", None, None),
        P("replica", "mp", None),
        P("replica", "mp"),
        P("mp", None),
        P("mp", None),
        P("mp"),
        P("replica", "mp"),
    )
    out_specs = (
        P("replica", "mp"),
        P(("mp", "replica"), None),
        P(("mp", "replica"), None),
        P(("mp", "replica")),
        P("mp", "replica", None),
    )
    return jax.shard_map(body, mesh=mesh, in_specs=in_specs, out_specs=out_specs, check_vma=False)
```
